32 devices in a mesh: tok: 16 (over z, x, core), head: 2 (over y).
Axes of the slice: x: 2, y: 2, z: 4, core: 2. Of those that a mesh axis runs over, the one named last changes fastest.
Arguments:
- tokens: bfloat16 [2048, 2560], P('tok', 'head'), may hold values from -6 to 6
- query_weight: bfloat16 [2560, 2560], P('tok'), may hold values from -0.125 to 0.125
- keyvalue_weight: bfloat16 [2560, 512], P('tok'), may hold values from -0.125 to 0.125
- output_weight: bfloat16 [2560, 2560], P(None, ('head', 'tok')), may hold values from -0.125 to 0.125
- cache: bfloat16 [128, 2, 128, 256], P(('tok', 'head')), may hold values from -460 to 460
- page_table: int32 [32, 4], P('tok'), may hold values from 0 to 127, as said below
- parents: int32 [32, 64], P('tok'), may hold values from 0 to 62, as said below
- cache_len: int32 [32], P('tok'), may hold values from 1 to 448, as said below
- accepted_leaf: int32 [32], P('tok'), may hold values from 0 to 63
Outputs:
- attended: bfloat16 [2048, 2560], P('tok', 'head')
- cache_out: bfloat16 [128, 2, 128, 256], P(('tok', 'head'))
The draws below stay inside these ranges and needn't reach their ends.
Inputs may be any that keep to these rules, and one draw needn't show every extreme that they name: `page_table`: for every d, row d names each of the pages d * 4 to d * 4 + 3 exactly once, so request d's pages all lie on device d (devices counted tok-major, head-minor). parents[r, 0] = 0, and parents[r, i] < i for i >= 1. `cache_len`: roughly half of the requests hold at most 128 cached positions, the others more than 320.
All inputs are finite; a program needn't handle non-finite values.
Results may differ from the reference program's by a relative error of at most 0.014.
The reference program's roundings to bfloat16 on the way count: a program that leaves them out, or rounds other values in their place, can miss the bound.
Values may be sent and summed in bfloat16 or wider, within the bound.
A program may use at most 64 MiB of HBM per device.

```python
import math
import jax
import jax.numpy as jnp
from jax import lax

D = 2560
HQ = 10
HD = 256
DRAFT = 64
PAGE = 128
NPR = 4
WINDOW = 256
REQ_DEV = 1
P_DEV = 4
CL_MAX = 448
REQUESTS = 32
TOKENS = 2048
PAGES = 128
N_HEAD = 2


def draw_cache(key, part):
    shape = (PAGES, 2, PAGE, HD)
    return jnp.clip(jax.random.normal(key, shape, jnp.float32), -6.0, 6.0).astype(jnp.bfloat16)


def draw_page_table(key, part):
    device_count = REQUESTS // REQ_DEV
    streams = jax.random.split(key, device_count)

    def shuffle(stream):
        return jax.random.permutation(stream, P_DEV)
    shuffled = jax.vmap(shuffle)(streams)
    offsets = jnp.arange(device_count, dtype=jnp.int32) * P_DEV
    return (shuffled.astype(jnp.int32) + offsets[:, None]).reshape(REQUESTS, NPR)


def draw_parents(key, part):
    node_ids = jnp.arange(DRAFT, dtype=jnp.int32)
    lowest = jnp.maximum(node_ids - 4, 0)
    offset = jax.random.randint(key, (REQUESTS, DRAFT), 0, 4)
    window_span = jnp.maximum(node_ids - lowest, 1)
    parent = lowest[None, :] + offset % window_span[None, :]
    parent = jnp.where(node_ids[None, :] == 0, 0, parent)
    return parent.at[0, DRAFT - 1].set(DRAFT - 2).astype(jnp.int32)


def draw_cache_len(key, part):
    streams = jax.random.split(key, 3)
    is_long = jax.random.permutation(streams[0], REQUESTS) < REQUESTS // 2
    short_len = jax.random.randint(streams[1], (REQUESTS,), 1, PAGE + 1)
    long_len = jax.random.randint(streams[2], (REQUESTS,), CL_MAX - PAGE + 1, CL_MAX + 1)
    lengths = jnp.where(is_long, long_len, short_len)
    return lengths.at[0].set(CL_MAX).at[1].set(1).astype(jnp.int32)


def draw_accepted_leaf(key, part):
    leaves = jax.random.randint(key, (REQUESTS,), 0, DRAFT)
    return leaves.at[0].set(DRAFT - 1).at[1].set(0).astype(jnp.int32)


def levels(own_key, dims, shards, smallest, largest):
    factor_of, own = 1.0, jax.random.fold_in(own_key, 6)
    for axis_at, parts in shards:
        steps = jnp.exp(jax.random.uniform(jax.random.fold_in(own, axis_at), (parts,), jnp.float32, smallest / len(shards), largest / len(shards)))
        factor_of = factor_of * jnp.repeat(steps, dims[axis_at] // parts).reshape([-1 if axis == axis_at else 1 for axis in range(len(dims))])
    return factor_of


def noise(rng, dims, deviation, most, pieces=(), kind=jnp.bfloat16):
    level = levels(rng, dims, pieces, -0.22, 0.18) if pieces else 1.0
    drawn = jax.random.normal(rng, dims, jnp.float32) * deviation * level
    return jnp.minimum(jnp.maximum(drawn, -most), most).astype(kind)


def setup_inputs(seed: int = 0) -> dict:
    keys = jax.random.split(jax.random.key(seed), 10)
    return {
        "tokens": noise(keys[0], (TOKENS, D), 1.0, 6.0, ((0, 16), (1, 2))),
        "query_weight": noise(keys[1], (D, HQ * HD), D ** -0.5, 0.125, ((0, 16),)),
        "keyvalue_weight": noise(keys[2], (D, 2 * HD), D ** -0.5, 0.125, ((0, 16),)),
        "output_weight": noise(keys[3], (HQ * HD, D), (HQ * HD) ** -0.5, 0.125, ((1, 32),)),
        "cache": draw_cache(jax.random.fold_in(keys[9], 71), 0),
        "page_table": draw_page_table(jax.random.fold_in(keys[9], 71), 0),
        "parents": draw_parents(jax.random.fold_in(keys[9], 71), 0),
        "cache_len": draw_cache_len(jax.random.fold_in(keys[9], 71), 0),
        "accepted_leaf": draw_accepted_leaf(jax.random.fold_in(keys[9], 71), 0),
    }


def ancestry(parent_row):
    node_ids = jnp.arange(DRAFT, dtype=jnp.int32)
    link = (parent_row[:, None] == node_ids[None, :]).astype(jnp.float32)
    reach = jnp.minimum(link + jnp.eye(DRAFT, dtype=jnp.float32), 1.0)
    for sweep in range((DRAFT - 1).bit_length()):
        reach = jnp.minimum(jnp.dot(reach, reach, precision=lax.Precision.HIGHEST), 1.0)
    depth = (lax.optimization_barrier(jnp.sum(reach, axis=1)) - 1.0).astype(jnp.int32)
    return (reach, depth)

def rotate(values, position):
    half = HD // 4
    freq = jnp.exp(jnp.arange(half, dtype=jnp.float32) * (-2.0 * math.log(10000.0) / (HD // 2)))
    angle = position.astype(jnp.float32)[..., None] * freq
    cosine = jnp.cos(angle)
    sine = jnp.sin(angle)
    first = values[..., :half]
    second = values[..., half:2 * half]
    return jnp.concatenate([first * cosine - second * sine, second * cosine + first * sine, values[..., 2 * half:]], axis=-1)

def attend(queries, cache_keys, cache_values, tree_keys, tree_values, lengths, position, reach):
    window_span = cache_keys.shape[1]
    slot_ids = jnp.arange(window_span, dtype=jnp.int32)
    visible = (slot_ids[None, None, :] < lengths[:, None, None]) & (slot_ids[None, None, :] > position[:, :, None] - WINDOW)
    cache_scores = jnp.einsum('rnhd,rcd->rhnc', queries.astype(jnp.float32), cache_keys.astype(jnp.float32))
    tree_scores = jnp.einsum('rnhd,rmd->rhnm', queries.astype(jnp.float32), tree_keys.astype(jnp.float32))
    cache_scores = jnp.where(visible[:, None], cache_scores, -1e+30)
    tree_scores = jnp.where(reach[:, None] > 0.5, tree_scores, -1e+30)
    row_peak = jnp.maximum(lax.optimization_barrier(jnp.max(cache_scores, axis=-1)), lax.optimization_barrier(jnp.max(tree_scores, axis=-1)))[..., None]
    cache_weights = jnp.exp(cache_scores - row_peak)
    tree_weights = jnp.exp(tree_scores - row_peak)
    denominator = lax.optimization_barrier(jnp.sum(cache_weights, axis=-1, keepdims=True)) + lax.optimization_barrier(jnp.sum(tree_weights, axis=-1, keepdims=True))
    cache_weights = (cache_weights / denominator).astype(jnp.bfloat16)
    tree_weights = (tree_weights / denominator).astype(jnp.bfloat16)
    result = jnp.einsum('rhnc,rcd->rnhd', cache_weights.astype(jnp.float32), cache_values.astype(jnp.float32))
    result = result + jnp.einsum('rhnm,rmd->rnhd', tree_weights.astype(jnp.float32), tree_values.astype(jnp.float32))
    return result.astype(jnp.bfloat16)

def refresh(logical_pages, length, leaf, reach, depth, new_keys, new_values):
    count = logical_pages.shape[0] * logical_pages.shape[2]
    logical = jnp.transpose(logical_pages, (1, 0, 2, 3)).reshape(2, count, HD)
    slot_ids = jnp.arange(count, dtype=jnp.int32)
    on_path = reach[leaf]
    selector = ((on_path[None, :] > 0.5) & (depth[None, :] == slot_ids[:, None] - length)).astype(jnp.float32)
    placed_keys = jnp.dot(selector, new_keys.astype(jnp.float32), precision=lax.Precision.HIGHEST)
    placed_values = jnp.dot(selector, new_values.astype(jnp.float32), precision=lax.Precision.HIGHEST)
    placed = jnp.stack([placed_keys, placed_values]).astype(jnp.bfloat16)
    written = lax.optimization_barrier(jnp.sum(selector, axis=1)) > 0.5
    logical = jnp.where(written[None, :, None], placed, logical)
    return jnp.transpose(logical.reshape(2, logical_pages.shape[0], logical_pages.shape[2], HD), (1, 0, 2, 3))

def reference(tokens, query_weight, keyvalue_weight, output_weight, cache, page_table, parents, cache_len, accepted_leaf):
    wide = tokens.astype(jnp.float32)
    mean_square = lax.optimization_barrier(jnp.mean(wide * wide, axis=1, keepdims=True))
    normed = (wide * lax.rsqrt(mean_square + 1e-06)).astype(jnp.bfloat16)
    reach, depth = jax.vmap(ancestry)(parents)
    position = cache_len[:, None] + depth
    flat_pos = position.reshape(TOKENS)
    queries = jnp.dot(normed, query_weight, preferred_element_type=jnp.float32).reshape(TOKENS, HQ, HD)
    queries = (rotate(queries, flat_pos[:, None]) * HD ** (-0.5)).astype(jnp.bfloat16)
    queries = queries.reshape(REQUESTS, DRAFT, HQ, HD)
    projected = jnp.dot(normed, keyvalue_weight, preferred_element_type=jnp.float32)
    tree_keys = rotate(projected[:, :HD], flat_pos).astype(jnp.bfloat16).reshape(REQUESTS, DRAFT, HD)
    tree_values = projected[:, HD:].astype(jnp.bfloat16).reshape(REQUESTS, DRAFT, HD)

    def one_request(packed):
        query_block, key_block, value_block, table_row, length, pos_row, reach_block = packed
        page_blocks = jnp.take(cache, table_row, axis=0)
        cache_keys = page_blocks[:, 0].reshape(NPR * PAGE, HD)
        cache_values = page_blocks[:, 1].reshape(NPR * PAGE, HD)
        return attend(query_block[None], cache_keys[None], cache_values[None], key_block[None], value_block[None], length[None], pos_row[None], reach_block[None])[0]
    mixed = lax.map(one_request, (queries, tree_keys, tree_values, page_table, cache_len, position, reach))
    mixed = mixed.reshape(TOKENS, HQ, HD)
    per_group = (HQ + N_HEAD - 1) // N_HEAD
    head_rows = output_weight.reshape(HQ, HD, D)
    summed = jnp.zeros((TOKENS, D), jnp.float32)
    for group in range(N_HEAD):
        head_ids = [group + N_HEAD * slot for slot in range(per_group) if group + N_HEAD * slot < HQ]
        if head_ids:
            chosen = jnp.array(head_ids, dtype=jnp.int32)
            columns = jnp.take(mixed, chosen, axis=1).reshape(TOKENS, len(head_ids) * HD)
            weights = jnp.take(head_rows, chosen, axis=0).reshape(len(head_ids) * HD, D)
            partial_value = jnp.dot(columns, weights, preferred_element_type=jnp.float32).astype(jnp.bfloat16)
            summed = summed + partial_value.astype(jnp.float32)
    attended = summed.astype(jnp.bfloat16)

    def one_update(packed):
        table_row, length, leaf, reach_block, depth_row, key_block, value_block = packed
        page_blocks = jnp.take(cache, table_row, axis=0)
        return refresh(page_blocks, length, leaf, reach_block, depth_row, key_block, value_block)
    new_pages = lax.map(one_update, (page_table, cache_len, accepted_leaf, reach, depth, tree_keys, tree_values))
    cache_out = cache.at[page_table.reshape(-1)].set(new_pages.reshape(REQUESTS * NPR, 2, PAGE, HD))
    return (attended, cache_out)
```

```python
import math

import jax
import jax.numpy as jnp
from jax import lax
from jax.experimental import pallas as pl
from jax.experimental.pallas import tpu as pltpu
from jax.sharding import PartitionSpec as P

HQ = 10
HD = 256
DRAFT = 64
PAGE = 128
NPR = 4
WINDOW = 256
CORES = 2
XS = 2
TILE = 16
MESH = pl.DeviceIdType.MESH
NT = (((1,), (1,)), ((), ()))


def ancestry(parent_row):
    node_ids = jnp.arange(DRAFT, dtype=jnp.int32)
    link = (parent_row[:, None] == node_ids[None, :]).astype(jnp.float32)
    reach = jnp.minimum(link + jnp.eye(DRAFT, dtype=jnp.float32), 1.0)
    for sweep in range((DRAFT - 1).bit_length()):
        reach = jnp.minimum(jnp.dot(reach, reach, precision=lax.Precision.HIGHEST), 1.0)
    depth = (jnp.sum(reach, axis=1) - 1.0).astype(jnp.int32)
    return (reach, depth)


def rotate(values, position):
    half = HD // 4
    freq = jnp.exp(jnp.arange(half, dtype=jnp.float32) * (-2.0 * math.log(10000.0) / (HD // 2)))
    angle = position.astype(jnp.float32)[..., None] * freq
    cosine = jnp.cos(angle)
    sine = jnp.sin(angle)
    first = values[..., :half]
    second = values[..., half : 2 * half]
    return jnp.concatenate(
        [first * cosine - second * sine, second * cosine + first * sine, values[..., 2 * half :]],
        axis=-1,
    )


def attend(queries, cache_keys, cache_values, tree_keys, tree_values, lengths, position, reach):
    window_span = cache_keys.shape[1]
    slot_ids = jnp.arange(window_span, dtype=jnp.int32)
    visible = (slot_ids[None, None, :] < lengths[:, None, None]) & (
        slot_ids[None, None, :] > position[:, :, None] - WINDOW
    )
    cache_scores = jnp.einsum(
        "rnhd,rcd->rhnc", queries, cache_keys, preferred_element_type=jnp.float32
    )
    tree_scores = jnp.einsum(
        "rnhd,rmd->rhnm", queries, tree_keys, preferred_element_type=jnp.float32
    )
    cache_scores = jnp.where(visible[:, None], cache_scores, -1e30)
    tree_scores = jnp.where(reach[:, None] > 0.5, tree_scores, -1e30)
    row_peak = jnp.maximum(jnp.max(cache_scores, axis=-1), jnp.max(tree_scores, axis=-1))[..., None]
    cache_weights = jnp.exp(cache_scores - row_peak)
    tree_weights = jnp.exp(tree_scores - row_peak)
    denominator = jnp.sum(cache_weights, axis=-1, keepdims=True) + jnp.sum(
        tree_weights, axis=-1, keepdims=True
    )
    cache_weights = (cache_weights / denominator).astype(jnp.bfloat16)
    tree_weights = (tree_weights / denominator).astype(jnp.bfloat16)
    result = jnp.einsum(
        "rhnc,rcd->rnhd", cache_weights, cache_values, preferred_element_type=jnp.float32
    )
    result = result + jnp.einsum(
        "rhnm,rmd->rnhd", tree_weights, tree_values, preferred_element_type=jnp.float32
    )
    return result.astype(jnp.bfloat16)


def refresh(logical_pages, length, leaf, reach, depth, new_keys, new_values):
    count = logical_pages.shape[0] * logical_pages.shape[2]
    logical = jnp.transpose(logical_pages, (1, 0, 2, 3)).reshape(2, count, HD)
    slot_ids = jnp.arange(count, dtype=jnp.int32)
    on_path = reach[leaf]
    selector = ((on_path[None, :] > 0.5) & (depth[None, :] == slot_ids[:, None] - length)).astype(
        jnp.float32
    )
    placed_keys = jnp.dot(selector, new_keys.astype(jnp.float32), precision=lax.Precision.HIGHEST)
    placed_values = jnp.dot(
        selector, new_values.astype(jnp.float32), precision=lax.Precision.HIGHEST
    )
    placed = jnp.stack([placed_keys, placed_values]).astype(jnp.bfloat16)
    written = jnp.sum(selector, axis=1) > 0.5
    logical = jnp.where(written[None, :, None], placed, logical)
    return jnp.transpose(
        logical.reshape(2, logical_pages.shape[0], logical_pages.shape[2], HD), (1, 0, 2, 3)
    )


def contract(source, piece):
    return jnp.dot(source, piece, preferred_element_type=jnp.float32)


def project_memory(rows, keyvalue_weight, position):
    projected = contract(rows, lax.all_gather(keyvalue_weight, "tok", axis=0, tiled=True))
    new_keys = rotate(projected[:, :HD], position).astype(jnp.bfloat16)
    new_values = projected[:, HD:].astype(jnp.bfloat16)
    return (new_keys, new_values)


def split_pages(page_blocks, count):
    cache_keys = page_blocks[:, :, 0].reshape(count, NPR * PAGE, HD)
    cache_values = page_blocks[:, :, 1].reshape(count, NPR * PAGE, HD)
    return (cache_keys, cache_values)


def reduce_heads(mixed, output_weight, safe_heads, head_mask, slots_per):
    head_count = lax.axis_size("head")
    tok_count = lax.axis_size("tok")
    narrow = output_weight.shape[1]
    blocks = lax.all_gather(output_weight, "head", axis=1, tiled=True)
    part_cols = blocks.shape[1]
    my_output_weight = (
        jnp.take(blocks.reshape(HQ, HD, part_cols), safe_heads, axis=0) * head_mask[:, None, None]
    )
    my_output_weight = my_output_weight.reshape(slots_per * HD, part_cols)
    partial_value = jnp.dot(
        mixed,
        lax.all_gather(my_output_weight, "tok", axis=1, tiled=True),
        preferred_element_type=jnp.float32,
    ).astype(jnp.bfloat16)
    row_count = partial_value.shape[0]
    partial_value = partial_value.reshape(row_count, tok_count, head_count, narrow)
    partial_value = jnp.transpose(partial_value, (0, 2, 1, 3)).reshape(
        row_count, tok_count * head_count * narrow
    )
    partial_value = lax.optimization_barrier(partial_value)
    summed = lax.psum_scatter(
        partial_value.astype(jnp.float32).astype(jnp.bfloat16),
        "head",
        scatter_dimension=1,
        tiled=True,
    )
    return summed


def shards(
    tokens,
    query_weight,
    keyvalue_weight,
    output_weight,
    cache,
    page_table,
    parents,
    cache_len,
    accepted_leaf,
):
    head_count = lax.axis_size("head")
    head_index = lax.axis_index("head")
    tok_index = lax.axis_index("tok")
    slots_per = -(-HQ // head_count)
    requests = parents.shape[0]
    owned = requests // head_count
    rows_owned = owned * DRAFT
    pages_dev = cache.shape[0]
    gathered = lax.all_gather(tokens, "head", axis=1, tiled=True)
    wide = gathered.astype(jnp.float32)
    mean_square = jnp.mean(wide * wide, axis=1, keepdims=True)
    normed = (wide * lax.rsqrt(mean_square + 1e-06)).astype(jnp.bfloat16)
    reach, depth = jax.vmap(ancestry)(parents)
    position = cache_len[:, None] + depth
    flat_pos = position.reshape(-1)
    head_ids = head_index + head_count * jnp.arange(slots_per, dtype=jnp.int32)
    usable = head_ids < HQ
    safe_heads = jnp.minimum(head_ids, HQ - 1)
    head_mask = usable.astype(jnp.bfloat16)
    part_rows = query_weight.shape[0]
    my_query_weight = (
        jnp.take(query_weight.reshape(part_rows, HQ, HD), safe_heads, axis=1)
        * head_mask[None, :, None]
    )
    my_query_weight = my_query_weight.reshape(part_rows, slots_per * HD)
    queries = contract(normed, lax.all_gather(my_query_weight, "tok", axis=0, tiled=True))
    queries = (rotate(queries.reshape(-1, slots_per, HD), flat_pos[:, None]) * HD ** (-0.5)).astype(
        jnp.bfloat16
    )
    own_start = head_index * rows_owned
    own_reach = lax.dynamic_slice_in_dim(reach, head_index * owned, owned, 0)
    own_depth = lax.dynamic_slice_in_dim(depth, head_index * owned, owned, 0)
    own_len = lax.dynamic_slice_in_dim(cache_len, head_index * owned, owned, 0)
    own_leaf = lax.dynamic_slice_in_dim(accepted_leaf, head_index * owned, owned, 0)
    device = tok_index * head_count + head_index
    own_table = (
        lax.dynamic_slice_in_dim(page_table, head_index * owned, owned, 0) - device * pages_dev
    )
    own_pages = jnp.take(cache, own_table.reshape(-1), axis=0).reshape(owned, NPR, 2, PAGE, HD)
    tree_keys, tree_values = project_memory(normed, keyvalue_weight, flat_pos)
    own_keys = lax.dynamic_slice_in_dim(tree_keys, own_start, rows_owned, 0)
    own_values = lax.dynamic_slice_in_dim(tree_values, own_start, rows_owned, 0)
    page_pool = lax.all_gather(cache, "head", axis=0, tiled=True)
    local_ids = page_table - tok_index * head_count * pages_dev
    page_blocks = jnp.take(page_pool, local_ids.reshape(-1), axis=0).reshape(
        requests, NPR, 2, PAGE, HD
    )
    cache_keys, cache_values = split_pages(page_blocks, requests)
    result = attend(
        queries.reshape(requests, DRAFT, slots_per, HD),
        cache_keys,
        cache_values,
        tree_keys.reshape(requests, DRAFT, HD),
        tree_values.reshape(requests, DRAFT, HD),
        cache_len,
        position,
        reach,
    )
    mixed = result.reshape(-1, slots_per * HD)
    attended = reduce_heads(mixed, output_weight, safe_heads, head_mask, slots_per)
    new_pages = jax.vmap(refresh)(
        own_pages,
        own_len,
        own_leaf,
        own_reach,
        own_depth,
        own_keys.reshape(owned, DRAFT, HD),
        own_values.reshape(owned, DRAFT, HD),
    )
    flat_ids = own_table.reshape(-1)
    matches = (flat_ids[:, None] == jnp.arange(pages_dev, dtype=jnp.int32)[None, :]).astype(
        jnp.int32
    )
    inverse = jnp.sum(matches * jnp.arange(pages_dev, dtype=jnp.int32)[:, None], axis=0)
    cache_out = jnp.take(new_pages.reshape(pages_dev, 2, PAGE, HD), inverse, axis=0)
    return (attended, cache_out)


def fused_kernel(
    tok_ref,
    qw_ref,
    kvw_ref,
    wo_ref,
    cache_ref,
    parents_ref,
    table_ref,
    len_ref,
    leaf_ref,
    out_ref,
    cache_out_ref,
    wbuf,
    obuf,
    osend,
    xbuf,
    cbuf,
    kvbuf,
    qbuf,
    mixbuf,
    reach_buf,
    depth_buf,
    psend,
    precv,
    y_send,
    y_recv,
    *piece_sems,
):
    tok_count = wbuf.shape[0]
    levels = tok_count // (XS * CORES)
    slots = qbuf.shape[0]
    rows = tok_ref.shape[0]
    half = tok_ref.shape[1]
    narrow = wo_ref.shape[0]
    main_rows = narrow - TILE
    requests = parents_ref.shape[0]
    qcols = slots * HD
    me = lax.axis_index("tok")
    y = lax.axis_index("head")
    other = 1 - y
    core = lax.rem(me, CORES)
    xpos = lax.rem(lax.div(me, CORES), XS)
    z = lax.div(me, CORES * XS)

    def tok_at(zz, xx, cc):
        return (zz * XS + xx) * CORES + cc

    up_dev = (jnp.minimum(me + XS * CORES, tok_count - 1), y)
    down_dev = (jnp.maximum(me - XS * CORES, 0), y)
    x_dev = (tok_at(z, 1 - xpos, core), y)
    core_dev = (tok_at(z, xpos, 1 - core), y)
    y_dev = (me, other)
    has_up = z < levels - 1
    has_down = z > 0

    barrier = pltpu.get_barrier_semaphore()
    for device in (x_dev, core_dev, y_dev):
        pl.semaphore_signal(barrier, inc=1, device_id=device, device_id_type=MESH)

    @pl.when(has_up)
    def _():
        pl.semaphore_signal(barrier, inc=1, device_id=up_dev, device_id_type=MESH)

    @pl.when(has_down)
    def _():
        pl.semaphore_signal(barrier, inc=1, device_id=down_dev, device_id_type=MESH)

    for slot in range(slots):
        source = pl.ds(pl.multiple_of((2 * slot + y) * HD, HD), HD)
        wbuf[me, :, slot * HD : (slot + 1) * HD] = qw_ref[:, source]
    wbuf[me, :, qcols:] = kvw_ref[:, pl.ds(pl.multiple_of(y * HD, HD), HD)]

    pl.semaphore_wait(barrier, 3 + has_up.astype(jnp.int32) + has_down.astype(jnp.int32))

    def remote(source, target, send_sem, recv_sem, device):
        return pltpu.make_async_remote_copy(
            src_ref=source,
            dst_ref=target,
            send_sem=send_sem,
            recv_sem=recv_sem,
            device_id=device,
            device_id_type=MESH,
        )

    class Piece:
        def __init__(self, view, sems, x_first):
            self.view = view
            self.up, self.down, self.xs, self.cs, self.recv = sems
            self.x_first = x_first

        def copy(self, t, sems, device):
            ref = self.view(t)
            return remote(ref, ref, sems.at[lax.div(t, CORES)], self.recv.at[t], device)

        def along(self, t, act, up, down):
            if up:
                pl.when(has_up)(lambda: act(self.copy(t, self.up, up_dev)))
            if down:
                pl.when(has_down)(lambda: act(self.copy(t, self.down, down_dev)))

        def spread(self, t, distance, own_x, act):
            if own_x and (not self.x_first or distance == 0):
                act(self.copy(t, self.xs, x_dev))
            act(self.copy(t, self.cs, core_dev))

        def arrive(self, t):
            self.copy(t, self.cs, core_dev).wait_recv()

        def visit(self, distance, sending, act):
            xs = (xpos, 1 - xpos) if self.x_first else (xpos,)
            for order, xx in enumerate(xs):
                if distance == 0:
                    t = tok_at(z, xx, core)
                    if sending and order == 1:
                        self.arrive(t)
                    self.along(t, act, True, True)
                    self.spread(t, 0, order == 0, act)
                    continue

                @pl.when(z - distance >= 0)
                def _():
                    t = tok_at(z - distance, xx, core)
                    if sending:
                        self.arrive(t)
                    self.along(t, act, True, False)
                    self.spread(t, distance, order == 0, act)

                @pl.when(z + distance < levels)
                def _():
                    t = tok_at(z + distance, xx, core)
                    if sending:
                        self.arrive(t)
                    self.along(t, act, False, True)
                    self.spread(t, distance, order == 0, act)

        def cross(self, distance, sending, act):
            if self.x_first:
                return
            targets = [z] if distance == 0 else [z - distance, z + distance]
            for index, zz in enumerate(targets):

                def go(zz=zz):
                    t = tok_at(zz, 1 - xpos, core)
                    if sending:
                        self.arrive(t)
                    self.spread(t, distance, False, act)

                if distance == 0:
                    go()
                else:
                    pl.when(zz >= 0 if index == 0 else zz < levels)(go)

        def step(self, distance):
            self.visit(distance, True, lambda copy: copy.start())

        def relay(self, distance):
            self.cross(distance, True, lambda copy: copy.start())

        def finish(self):
            for zz in range(levels):
                for xx in range(XS):
                    self.arrive(tok_at(zz, xx, 1 - core))

        def drain(self):
            for distance in range(levels):
                self.visit(distance, False, lambda copy: copy.wait_send())
                self.cross(distance, False, lambda copy: copy.wait_send())

    pieces = [piece_sems[5 * i : 5 * i + 5] for i in range(4)]
    q_piece = Piece(lambda t: wbuf.at[t, :, :qcols], pieces[0], False)
    k_piece = Piece(lambda t: wbuf.at[t, :, qcols:], pieces[1], True)
    o_piece = Piece(lambda t: obuf.at[:, t, :main_rows], pieces[2], False)
    s_piece = Piece(lambda t: obuf.at[:, t, main_rows:], pieces[3], True)

    def step(group, distance):
        for piece in group:
            piece.step(distance)

    def relay(group, distance):
        for piece in group:
            piece.relay(distance)

    weights = (q_piece, k_piece)
    outputs = (o_piece, s_piece)

    q_piece.step(0)

    xsend = remote(tok_ref, xbuf.at[y], y_send.at[0], y_recv.at[0], y_dev)
    xsend.start()
    for slot in range(slots):
        source = pl.ds(pl.multiple_of((2 * slot + other) * HD, HD), HD)
        osend[:, slot * HD : (slot + 1) * HD] = wo_ref[:, source]
    wosend = remote(osend, obuf.at[y, me], y_send.at[1], y_recv.at[1], y_dev)
    wosend.start()
    csend = remote(cache_ref, cbuf.at[y], y_send.at[2], y_recv.at[2], y_dev)
    csend.start()
    for slot in range(slots):
        source = pl.ds(pl.multiple_of((2 * slot + y) * HD, HD), HD)
        obuf[y, me, :, slot * HD : (slot + 1) * HD] = wo_ref[:, source]
    xbuf[y] = tok_ref[...]
    cbuf[y] = cache_ref[...]

    k_piece.step(0)

    row_ids = lax.broadcasted_iota(jnp.int32, (DRAFT, DRAFT), 0)
    col_ids = lax.broadcasted_iota(jnp.int32, (DRAFT, DRAFT), 1)
    eye = (row_ids == col_ids).astype(jnp.float32)
    lane = lax.broadcasted_iota(jnp.int32, (1, HD // 2), 1)
    quarter = HD // 4
    pair = jnp.where(lane < quarter, lane, lane - quarter).astype(jnp.float32)
    freq = jnp.exp(pair * (-2.0 * math.log(10000.0) / (HD // 2)))
    sign = jnp.where(lane < quarter, -1.0, 1.0)
    reaches = []
    positions = []
    for r in range(requests):
        back = (row_ids == parents_ref[r : r + 1, :]).astype(jnp.float32)
        back = jnp.minimum(back + eye, 1.0)
        for sweep in range((DRAFT - 1).bit_length()):
            low = back.astype(jnp.bfloat16)
            back = jnp.minimum(jnp.dot(low, low, preferred_element_type=jnp.float32), 1.0)
        reach = lax.dot_general(
            eye.astype(jnp.bfloat16),
            back.astype(jnp.bfloat16),
            NT,
            preferred_element_type=jnp.float32,
        )
        reach_buf[r] = reach
        depth_buf[r] = jnp.sum(back, axis=0, keepdims=True) - 1.0
        reaches.append(reach)
        depth = jnp.sum(reach, axis=1, keepdims=True) - 1.0
        positions.append(depth + len_ref[r].astype(jnp.float32))
    angle = jnp.concatenate(positions, axis=0) * freq
    cosine = jnp.cos(angle)
    sine = jnp.sin(angle) * sign

    def rotated(value):
        turn = value[:, : HD // 2]
        swapped = jnp.concatenate([turn[:, quarter:], turn[:, :quarter]], axis=1)
        return jnp.concatenate([turn * cosine + swapped * sine, value[:, HD // 2 :]], axis=1)

    step(weights, 1)
    relay(weights, 0)
    xsend.wait_recv()
    wide = jnp.concatenate([xbuf[0], xbuf[1]], axis=1).astype(jnp.float32)
    mean_square = jnp.mean(wide * wide, axis=1, keepdims=True)
    normed = (wide * lax.rsqrt(mean_square + 1e-06)).astype(jnp.bfloat16)

    for distance in range(2, levels):
        step(weights, distance)
        relay(weights, distance - 1)
        if distance == 2:
            wosend.wait_recv()
            step(outputs, 0)
    step(outputs, 1)
    relay(weights, levels - 1)
    for piece in weights:
        piece.finish()

    def project(start):
        block = wbuf[:, :, start : start + HD].reshape(-1, HD)
        return jnp.dot(normed, block, preferred_element_type=jnp.float32)

    projected = project(qcols)

    @pl.when(y == 0)
    def _():
        kvbuf[0] = rotated(projected).astype(jnp.bfloat16)

    @pl.when(y == 1)
    def _():
        kvbuf[1] = projected.astype(jnp.bfloat16)

    kvsend = remote(kvbuf.at[y], kvbuf.at[y], y_send.at[3], y_recv.at[3], y_dev)
    kvsend.start()
    for slot in range(slots):
        qbuf[slot] = (rotated(project(slot * HD)) * HD ** (-0.5)).astype(jnp.bfloat16)
    relay(outputs, 0)
    kvsend.wait_recv()
    csend.wait_recv()

    def attend_one(r):
        span = slice(r * DRAFT, (r + 1) * DRAFT)
        queries = qbuf[:, span, :].reshape(slots * DRAFT, HD)
        ids = [lax.rem(table_ref[r, j], NPR) for j in range(NPR)]
        keys = jnp.concatenate([cbuf[r, i, 0] for i in ids], axis=0)
        values = jnp.concatenate([cbuf[r, i, 1] for i in ids], axis=0)
        span_len = NPR * PAGE
        slot_ids = lax.broadcasted_iota(jnp.int32, (DRAFT, span_len), 1)
        first = positions[r].astype(jnp.int32) - WINDOW
        visible = (slot_ids < len_ref[r]) & (slot_ids > first)
        cache_bias = jnp.where(visible, 0.0, -1e30)
        tree_bias = jnp.where(reaches[r] > 0.5, 0.0, -1e30)
        scores = lax.dot_general(queries, keys, NT, preferred_element_type=jnp.float32)
        tree = lax.dot_general(queries, kvbuf[0, span, :], NT, preferred_element_type=jnp.float32)
        scores = jnp.where(cache_bias[None] < 0.0, -1e30, scores.reshape(slots, DRAFT, span_len))
        tree = jnp.where(tree_bias[None] < 0.0, -1e30, tree.reshape(slots, DRAFT, DRAFT))
        peak = jnp.maximum(
            jnp.max(scores, axis=-1, keepdims=True), jnp.max(tree, axis=-1, keepdims=True)
        )
        scores = jnp.exp(scores - peak)
        tree = jnp.exp(tree - peak)
        total = jnp.sum(scores, axis=-1, keepdims=True) + jnp.sum(tree, axis=-1, keepdims=True)
        scores = (scores / total).astype(jnp.bfloat16).reshape(slots * DRAFT, span_len)
        tree = (tree / total).astype(jnp.bfloat16).reshape(slots * DRAFT, DRAFT)
        result = jnp.dot(scores, values, preferred_element_type=jnp.float32)
        result = result + jnp.dot(tree, kvbuf[1, span, :], preferred_element_type=jnp.float32)
        result = result.astype(jnp.bfloat16)
        for slot in range(slots):
            mixbuf[span, slot * HD : (slot + 1) * HD] = result[slot * DRAFT : (slot + 1) * DRAFT]

    def refresh_one():
        length = len_ref[y]
        own_reach = reach_buf[y]
        on_path = jnp.sum(jnp.where(row_ids == leaf_ref[y], own_reach, 0.0), axis=0, keepdims=True)
        depth_row = depth_buf[y].astype(jnp.int32)
        keep = pl.ds(pl.multiple_of(y * DRAFT, DRAFT), DRAFT)
        new_keys = kvbuf[0, keep, :]
        new_values = kvbuf[1, keep, :]
        slot_ids = lax.broadcasted_iota(jnp.int32, (PAGE, DRAFT), 0)
        for page in range(NPR):
            logical = jnp.int32(0)
            for j in range(1, NPR):
                logical = logical + jnp.where(lax.rem(table_ref[y, j], NPR) == page, j, 0)
            chosen = (on_path > 0.5) & (depth_row == slot_ids + (logical * PAGE - length))
            selector = chosen.astype(jnp.float32)
            written = jnp.sum(selector, axis=1, keepdims=True) > 0.5
            selector = selector.astype(jnp.bfloat16)
            for entry, new in ((0, new_keys), (1, new_values)):
                placed = jnp.dot(selector, new, preferred_element_type=jnp.float32)
                old = cache_ref[page, entry].astype(jnp.float32)
                cache_out_ref[page, entry] = jnp.where(written, placed, old).astype(jnp.bfloat16)

    step(outputs, 2) if levels > 2 else None
    relay(outputs, 1)
    attend_one(0)
    for distance in range(3, levels):
        step(outputs, distance)
        relay(outputs, distance - 1)
    for r in range(1, requests):
        attend_one(r)
    refresh_one()
    relay(outputs, levels - 1)
    for piece in outputs:
        piece.finish()

    mixed = mixbuf[...]
    part = tok_count // 2
    width = part * narrow
    sends = []
    for index in range(2):
        block = obuf[other, index * part : (index + 1) * part].reshape(width, qcols)
        value = lax.dot_general(mixed, block, NT, preferred_element_type=jnp.float32)
        psend[index] = value.astype(jnp.bfloat16)
        copy = remote(
            psend.at[index], precv.at[index], y_send.at[4 + index], y_recv.at[4 + index], y_dev
        )
        copy.start()
        sends.append(copy)
    for index in range(2):
        block = obuf[y, index * part : (index + 1) * part].reshape(width, qcols)
        value = lax.dot_general(mixed, block, NT, preferred_element_type=jnp.float32)
        value = value.astype(jnp.bfloat16).astype(jnp.float32)
        sends[index].wait_recv()
        summed = value + precv[index].astype(jnp.float32)
        out_ref[:, index * width : (index + 1) * width] = summed.astype(jnp.bfloat16)
    for piece in weights + outputs:
        piece.drain()
    for copy in [xsend, wosend, csend, kvsend] + sends:
        copy.wait_send()


def fused(tokens, query_weight, keyvalue_weight, output_weight, cache, page_table, parents, cache_len, accepted_leaf):
    tok_count = lax.axis_size("tok")
    heads = lax.axis_size("head")
    slots = HQ // heads
    rows, half = tokens.shape
    part_rows = query_weight.shape[0]
    narrow = output_weight.shape[1]
    requests = parents.shape[0]
    pages = cache.shape[0]
    qcols = slots * HD
    positions = tok_count // CORES
    vmem = pl.BlockSpec(memory_space=pltpu.VMEM)
    smem = pl.BlockSpec(memory_space=pltpu.SMEM)
    bf16 = jnp.bfloat16
    scratch = [
        pltpu.VMEM((tok_count, part_rows, qcols + HD), bf16),
        pltpu.VMEM((heads, tok_count, narrow, qcols), bf16),
        pltpu.VMEM((narrow, qcols), bf16),
        pltpu.VMEM((heads, rows, half), bf16),
        pltpu.VMEM((heads,) + cache.shape, bf16),
        pltpu.VMEM((2, rows, HD), bf16),
        pltpu.VMEM((slots, rows, HD), bf16),
        pltpu.VMEM((rows, qcols), bf16),
        pltpu.VMEM((requests, DRAFT, DRAFT), jnp.float32),
        pltpu.VMEM((requests, 1, DRAFT), jnp.float32),
        pltpu.VMEM((2, rows, half // 2), bf16),
        pltpu.VMEM((2, rows, half // 2), bf16),
        pltpu.SemaphoreType.DMA((6,)),
        pltpu.SemaphoreType.DMA((6,)),
    ]
    for piece in range(4):
        scratch += [pltpu.SemaphoreType.DMA((positions,))] * 4
        scratch += [pltpu.SemaphoreType.DMA((tok_count,))]
    return pl.pallas_call(
        fused_kernel,
        out_shape=(
            jax.ShapeDtypeStruct(tokens.shape, bf16),
            jax.ShapeDtypeStruct(cache.shape, bf16),
        ),
        in_specs=[vmem] * 6 + [smem] * 3,
        out_specs=(vmem, vmem),
        scratch_shapes=scratch,
        compiler_params=pltpu.CompilerParams(
            collective_id=0, has_side_effects=True, vmem_limit_bytes=48 * 1024 * 1024
        ),
        cost_estimate=pl.CostEstimate(
            flops=4 * rows * HD * HQ * HD * 5, bytes_accessed=1 << 22, transcendentals=1 << 19
        ),
    )(
        tokens,
        query_weight,
        keyvalue_weight,
        jnp.transpose(output_weight),
        cache,
        parents,
        page_table,
        cache_len,
        accepted_leaf,
    )


def fits(tok_count, head_count, args):
    tokens, query_weight, _, output_weight, cache, _, parents, _, _ = args
    return (
        head_count == 2
        and tok_count % (2 * XS * CORES) == 0
        and tok_count >= 3 * XS * CORES
        and query_weight.shape[0] % TILE == 0
        and output_weight.shape[1] % TILE == 0
        and output_weight.shape[1] > TILE
        and (tokens.shape[1] // 2) % 128 == 0
        and cache.shape[0] == NPR
        and parents.shape[0] == head_count
    )


def dispatch(*args):
    if fits(lax.axis_size("tok"), lax.axis_size("head"), args):
        return fused(*args)
    return shards(*args)


def solution(mesh):
    in_specs = (
        P("tok", "head"),
        P("tok", None),
        P("tok", None),
        P(None, ("head", "tok")),
        P(("tok", "head"), None, None, None),
        P("tok", None),
        P("tok", None),
        P("tok"),
        P("tok"),
    )
    out_specs = (P("tok", "head"), P(("tok", "head"), None, None, None))
    return jax.shard_map(
        dispatch, mesh=mesh, in_specs=in_specs, out_specs=out_specs, check_vma=False
    )
```

```python
import math

import jax
import jax.numpy as jnp
from jax import lax
from jax.experimental import pallas as pl
from jax.experimental.pallas import tpu as pltpu
from jax.sharding import PartitionSpec as P

HQ = 10
HD = 256
DRAFT = 64
PAGE = 128
NPR = 4
WINDOW = 256
CORES = 2
XS = 2
TILE = 16
MESH = pl.DeviceIdType.MESH
NT = (((1,), (1,)), ((), ()))


def ancestry(parent_row):
    node_ids = jnp.arange(DRAFT, dtype=jnp.int32)
    link = (parent_row[:, None] == node_ids[None, :]).astype(jnp.float32)
    reach = jnp.minimum(link + jnp.eye(DRAFT, dtype=jnp.float32), 1.0)
    for sweep in range((DRAFT - 1).bit_length()):
        reach = jnp.minimum(jnp.dot(reach, reach, precision=lax.Precision.HIGHEST), 1.0)
    depth = (jnp.sum(reach, axis=1) - 1.0).astype(jnp.int32)
    return (reach, depth)


def rotate(values, position):
    half = HD // 4
    freq = jnp.exp(jnp.arange(half, dtype=jnp.float32) * (-2.0 * math.log(10000.0) / (HD // 2)))
    angle = position.astype(jnp.float32)[..., None] * freq
    cosine = jnp.cos(angle)
    sine = jnp.sin(angle)
    first = values[..., :half]
    second = values[..., half : 2 * half]
    return jnp.concatenate(
        [first * cosine - second * sine, second * cosine + first * sine, values[..., 2 * half :]],
        axis=-1,
    )


def attend(queries, cache_keys, cache_values, tree_keys, tree_values, lengths, position, reach):
    window_span = cache_keys.shape[1]
    slot_ids = jnp.arange(window_span, dtype=jnp.int32)
    visible = (slot_ids[None, None, :] < lengths[:, None, None]) & (
        slot_ids[None, None, :] > position[:, :, None] - WINDOW
    )
    cache_scores = jnp.einsum(
        "rnhd,rcd->rhnc", queries, cache_keys, preferred_element_type=jnp.float32
    )
    tree_scores = jnp.einsum(
        "rnhd,rmd->rhnm", queries, tree_keys, preferred_element_type=jnp.float32
    )
    cache_scores = jnp.where(visible[:, None], cache_scores, -1e30)
    tree_scores = jnp.where(reach[:, None] > 0.5, tree_scores, -1e30)
    row_peak = jnp.maximum(jnp.max(cache_scores, axis=-1), jnp.max(tree_scores, axis=-1))[..., None]
    cache_weights = jnp.exp(cache_scores - row_peak)
    tree_weights = jnp.exp(tree_scores - row_peak)
    denominator = jnp.sum(cache_weights, axis=-1, keepdims=True) + jnp.sum(
        tree_weights, axis=-1, keepdims=True
    )
    cache_weights = (cache_weights / denominator).astype(jnp.bfloat16)
    tree_weights = (tree_weights / denominator).astype(jnp.bfloat16)
    result = jnp.einsum(
        "rhnc,rcd->rnhd", cache_weights, cache_values, preferred_element_type=jnp.float32
    )
    result = result + jnp.einsum(
        "rhnm,rmd->rnhd", tree_weights, tree_values, preferred_element_type=jnp.float32
    )
    return result.astype(jnp.bfloat16)


def refresh(logical_pages, length, leaf, reach, depth, new_keys, new_values):
    count = logical_pages.shape[0] * logical_pages.shape[2]
    logical = jnp.transpose(logical_pages, (1, 0, 2, 3)).reshape(2, count, HD)
    slot_ids = jnp.arange(count, dtype=jnp.int32)
    on_path = reach[leaf]
    selector = ((on_path[None, :] > 0.5) & (depth[None, :] == slot_ids[:, None] - length)).astype(
        jnp.float32
    )
    placed_keys = jnp.dot(selector, new_keys.astype(jnp.float32), precision=lax.Precision.HIGHEST)
    placed_values = jnp.dot(
        selector, new_values.astype(jnp.float32), precision=lax.Precision.HIGHEST
    )
    placed = jnp.stack([placed_keys, placed_values]).astype(jnp.bfloat16)
    written = jnp.sum(selector, axis=1) > 0.5
    logical = jnp.where(written[None, :, None], placed, logical)
    return jnp.transpose(
        logical.reshape(2, logical_pages.shape[0], logical_pages.shape[2], HD), (1, 0, 2, 3)
    )


def contract(source, piece):
    return jnp.dot(source, piece, preferred_element_type=jnp.float32)


def project_memory(rows, keyvalue_weight, position):
    projected = contract(rows, lax.all_gather(keyvalue_weight, "tok", axis=0, tiled=True))
    new_keys = rotate(projected[:, :HD], position).astype(jnp.bfloat16)
    new_values = projected[:, HD:].astype(jnp.bfloat16)
    return (new_keys, new_values)


def split_pages(page_blocks, count):
    cache_keys = page_blocks[:, :, 0].reshape(count, NPR * PAGE, HD)
    cache_values = page_blocks[:, :, 1].reshape(count, NPR * PAGE, HD)
    return (cache_keys, cache_values)


def reduce_heads(mixed, output_weight, safe_heads, head_mask, slots_per):
    head_count = lax.axis_size("head")
    tok_count = lax.axis_size("tok")
    narrow = output_weight.shape[1]
    blocks = lax.all_gather(output_weight, "head", axis=1, tiled=True)
    part_cols = blocks.shape[1]
    my_output_weight = (
        jnp.take(blocks.reshape(HQ, HD, part_cols), safe_heads, axis=0) * head_mask[:, None, None]
    )
    my_output_weight = my_output_weight.reshape(slots_per * HD, part_cols)
    partial_value = jnp.dot(
        mixed,
        lax.all_gather(my_output_weight, "tok", axis=1, tiled=True),
        preferred_element_type=jnp.float32,
    ).astype(jnp.bfloat16)
    row_count = partial_value.shape[0]
    partial_value = partial_value.reshape(row_count, tok_count, head_count, narrow)
    partial_value = jnp.transpose(partial_value, (0, 2, 1, 3)).reshape(
        row_count, tok_count * head_count * narrow
    )
    partial_value = lax.optimization_barrier(partial_value)
    summed = lax.psum_scatter(
        partial_value.astype(jnp.float32).astype(jnp.bfloat16),
        "head",
        scatter_dimension=1,
        tiled=True,
    )
    return summed


def shards(
    tokens,
    query_weight,
    keyvalue_weight,
    output_weight,
    cache,
    page_table,
    parents,
    cache_len,
    accepted_leaf,
):
    head_count = lax.axis_size("head")
    head_index = lax.axis_index("head")
    tok_index = lax.axis_index("tok")
    slots_per = -(-HQ // head_count)
    requests = parents.shape[0]
    owned = requests // head_count
    rows_owned = owned * DRAFT
    pages_dev = cache.shape[0]
    gathered = lax.all_gather(tokens, "head", axis=1, tiled=True)
    wide = gathered.astype(jnp.float32)
    mean_square = jnp.mean(wide * wide, axis=1, keepdims=True)
    normed = (wide * lax.rsqrt(mean_square + 1e-06)).astype(jnp.bfloat16)
    reach, depth = jax.vmap(ancestry)(parents)
    position = cache_len[:, None] + depth
    flat_pos = position.reshape(-1)
    head_ids = head_index + head_count * jnp.arange(slots_per, dtype=jnp.int32)
    usable = head_ids < HQ
    safe_heads = jnp.minimum(head_ids, HQ - 1)
    head_mask = usable.astype(jnp.bfloat16)
    part_rows = query_weight.shape[0]
    my_query_weight = (
        jnp.take(query_weight.reshape(part_rows, HQ, HD), safe_heads, axis=1)
        * head_mask[None, :, None]
    )
    my_query_weight = my_query_weight.reshape(part_rows, slots_per * HD)
    queries = contract(normed, lax.all_gather(my_query_weight, "tok", axis=0, tiled=True))
    queries = (rotate(queries.reshape(-1, slots_per, HD), flat_pos[:, None]) * HD ** (-0.5)).astype(
        jnp.bfloat16
    )
    own_start = head_index * rows_owned
    own_reach = lax.dynamic_slice_in_dim(reach, head_index * owned, owned, 0)
    own_depth = lax.dynamic_slice_in_dim(depth, head_index * owned, owned, 0)
    own_len = lax.dynamic_slice_in_dim(cache_len, head_index * owned, owned, 0)
    own_leaf = lax.dynamic_slice_in_dim(accepted_leaf, head_index * owned, owned, 0)
    device = tok_index * head_count + head_index
    own_table = (
        lax.dynamic_slice_in_dim(page_table, head_index * owned, owned, 0) - device * pages_dev
    )
    own_pages = jnp.take(cache, own_table.reshape(-1), axis=0).reshape(owned, NPR, 2, PAGE, HD)
    tree_keys, tree_values = project_memory(normed, keyvalue_weight, flat_pos)
    own_keys = lax.dynamic_slice_in_dim(tree_keys, own_start, rows_owned, 0)
    own_values = lax.dynamic_slice_in_dim(tree_values, own_start, rows_owned, 0)
    page_pool = lax.all_gather(cache, "head", axis=0, tiled=True)
    local_ids = page_table - tok_index * head_count * pages_dev
    page_blocks = jnp.take(page_pool, local_ids.reshape(-1), axis=0).reshape(
        requests, NPR, 2, PAGE, HD
    )
    cache_keys, cache_values = split_pages(page_blocks, requests)
    result = attend(
        queries.reshape(requests, DRAFT, slots_per, HD),
        cache_keys,
        cache_values,
        tree_keys.reshape(requests, DRAFT, HD),
        tree_values.reshape(requests, DRAFT, HD),
        cache_len,
        position,
        reach,
    )
    mixed = result.reshape(-1, slots_per * HD)
    attended = reduce_heads(mixed, output_weight, safe_heads, head_mask, slots_per)
    new_pages = jax.vmap(refresh)(
        own_pages,
        own_len,
        own_leaf,
        own_reach,
        own_depth,
        own_keys.reshape(owned, DRAFT, HD),
        own_values.reshape(owned, DRAFT, HD),
    )
    flat_ids = own_table.reshape(-1)
    matches = (flat_ids[:, None] == jnp.arange(pages_dev, dtype=jnp.int32)[None, :]).astype(
        jnp.int32
    )
    inverse = jnp.sum(matches * jnp.arange(pages_dev, dtype=jnp.int32)[:, None], axis=0)
    cache_out = jnp.take(new_pages.reshape(pages_dev, 2, PAGE, HD), inverse, axis=0)
    return (attended, cache_out)


def fused_kernel(
    tok_ref,
    qw_ref,
    kvw_ref,
    wo_ref,
    cache_ref,
    parents_ref,
    table_ref,
    len_ref,
    leaf_ref,
    out_ref,
    cache_out_ref,
    wbuf,
    obuf,
    xbuf,
    cbuf,
    kvbuf,
    qbuf,
    mixbuf,
    reach_buf,
    depth_buf,
    nbuf,
    accum,
    psend,
    pown,
    precv,
    y_send,
    y_recv,
    part_send,
    part_recv,
    load_sem,
    *piece_sems,
):
    tok_count = wbuf.shape[0]
    levels = tok_count // (XS * CORES)
    slots = qbuf.shape[0]
    rows = tok_ref.shape[0]
    narrow = wo_ref.shape[0]
    main_rows = narrow - TILE
    requests = parents_ref.shape[0]
    level = XS * CORES
    part_rows = wbuf.shape[1]
    qcols = slots * HD
    me = lax.axis_index("tok")
    y = lax.axis_index("head")
    other = 1 - y
    core = lax.rem(me, CORES)
    xpos = lax.rem(lax.div(me, CORES), XS)
    z = lax.div(me, CORES * XS)

    def tok_at(zz, xx, cc):
        return (zz * XS + xx) * CORES + cc

    up_dev = (jnp.minimum(me + XS * CORES, tok_count - 1), y)
    down_dev = (jnp.maximum(me - XS * CORES, 0), y)
    x_dev = (tok_at(z, 1 - xpos, core), y)
    core_dev = (tok_at(z, xpos, 1 - core), y)
    y_dev = (me, other)
    has_up = z < levels - 1
    has_down = z > 0

    def columns(slot, group):
        return pl.ds(pl.multiple_of((2 * slot + group) * HD, HD), HD)

    loads = [
        (
            qw_ref.at[:, columns(slot, y)],
            wbuf.at[me, :, slot * HD : (slot + 1) * HD],
        )
        for slot in range(slots)
    ]
    loads.append((kvw_ref.at[:, pl.ds(pl.multiple_of(y * HD, HD), HD)], wbuf.at[me, :, qcols:]))
    weight_loads = len(loads)
    loads += [
        (
            wo_ref.at[:, columns(slot, y)],
            obuf.at[y, me, :, slot * HD : (slot + 1) * HD],
        )
        for slot in range(slots)
    ]
    loads += [(tok_ref, xbuf.at[y]), (cache_ref, cbuf.at[y])]
    loads = [
        pltpu.make_async_copy(source, target, load_sem.at[index])
        for index, (source, target) in enumerate(loads)
    ]
    for load in loads:
        load.start()

    barrier = pltpu.get_barrier_semaphore()
    for device in (x_dev, core_dev, y_dev):
        pl.semaphore_signal(barrier, inc=1, device_id=device, device_id_type=MESH)

    @pl.when(has_up)
    def _():
        pl.semaphore_signal(barrier, inc=1, device_id=up_dev, device_id_type=MESH)

    @pl.when(has_down)
    def _():
        pl.semaphore_signal(barrier, inc=1, device_id=down_dev, device_id_type=MESH)

    pl.semaphore_wait(barrier, 3 + has_up.astype(jnp.int32) + has_down.astype(jnp.int32))

    def remote(source, target, send_sem, recv_sem, device):
        return pltpu.make_async_remote_copy(
            src_ref=source,
            dst_ref=target,
            send_sem=send_sem,
            recv_sem=recv_sem,
            device_id=device,
            device_id_type=MESH,
        )

    class Piece:
        def __init__(self, view, sems, x_first):
            self.view = view
            self.up, self.down, self.xs, self.cs, self.recv = sems
            self.x_first = x_first

        def copy(self, t, sems, device):
            ref = self.view(t)
            return remote(ref, ref, sems.at[lax.div(t, CORES)], self.recv.at[t], device)

        def along(self, t, act, up, down):
            if up:
                pl.when(has_up)(lambda: act(self.copy(t, self.up, up_dev)))
            if down:
                pl.when(has_down)(lambda: act(self.copy(t, self.down, down_dev)))

        def spread(self, t, distance, own_x, act):
            if own_x and (not self.x_first or distance == 0):
                act(self.copy(t, self.xs, x_dev))
            act(self.copy(t, self.cs, core_dev))

        def arrive(self, t):
            self.copy(t, self.cs, core_dev).wait_recv()

        def visit(self, distance, sending, act, orders=(0, 1)):
            xs = (xpos, 1 - xpos) if self.x_first else (xpos,)
            for order, xx in enumerate(xs):
                if order not in orders:
                    continue
                if distance == 0:
                    t = tok_at(z, xx, core)
                    if sending and order == 1:
                        self.arrive(t)
                    self.along(t, act, True, True)
                    self.spread(t, 0, order == 0, act)
                    continue

                @pl.when(z - distance >= 0)
                def _():
                    t = tok_at(z - distance, xx, core)
                    if sending:
                        self.arrive(t)
                    self.along(t, act, True, False)
                    self.spread(t, distance, order == 0, act)

                @pl.when(z + distance < levels)
                def _():
                    t = tok_at(z + distance, xx, core)
                    if sending:
                        self.arrive(t)
                    self.along(t, act, False, True)
                    self.spread(t, distance, order == 0, act)

        def cross(self, distance, sending, act):
            if self.x_first:
                return
            targets = [z] if distance == 0 else [z - distance, z + distance]
            for index, zz in enumerate(targets):

                def go(zz=zz):
                    t = tok_at(zz, 1 - xpos, core)
                    if sending:
                        self.arrive(t)
                    self.spread(t, distance, False, act)

                if distance == 0:
                    go()
                else:
                    pl.when(zz >= 0 if index == 0 else zz < levels)(go)

        def step(self, distance, orders=(0, 1)):
            self.visit(distance, True, lambda copy: copy.start(), orders)

        def relay(self, distance):
            self.cross(distance, True, lambda copy: copy.start())

        def gathered(self, zz):
            for xx in range(XS):
                self.arrive(tok_at(zz, xx, 1 - core))

        def drain(self):
            for distance in range(levels):
                self.visit(distance, False, lambda copy: copy.wait_send())
                self.cross(distance, False, lambda copy: copy.wait_send())

    pieces = [piece_sems[5 * i : 5 * i + 5] for i in range(6)]
    cut = slots // 2 * HD
    mid = main_rows // 2 // TILE * TILE
    k_piece = Piece(lambda t: wbuf.at[t, :, qcols:], pieces[0], True)
    qa_piece = Piece(lambda t: wbuf.at[t, :, :cut], pieces[1], False)
    qb_piece = Piece(lambda t: wbuf.at[t, :, cut:qcols], pieces[2], False)
    oa_piece = Piece(lambda t: obuf.at[:, t, :mid], pieces[3], False)
    ob_piece = Piece(lambda t: obuf.at[:, t, mid:main_rows], pieces[4], False)
    s_piece = Piece(lambda t: obuf.at[:, t, main_rows:], pieces[5], True)

    def step(group, distance):
        for piece in group:
            piece.step(distance)

    def relay(group, distance):
        for piece in group:
            piece.relay(distance)

    def each_level(distance, run):
        if distance == 0:
            run(z)
            return
        pl.when(z - distance >= 0)(lambda: run(z - distance))
        pl.when(z + distance < levels)(lambda: run(z + distance))

    weights = (k_piece, qa_piece, qb_piece)
    outputs = (oa_piece, ob_piece, s_piece)

    wosends = [
        remote(
            wo_ref.at[:, columns(slot, other)],
            obuf.at[y, me, :, slot * HD : (slot + 1) * HD],
            y_send.at[3 + slot],
            y_recv.at[3 + slot],
            y_dev,
        )
        for slot in range(slots)
    ]
    xsend = remote(tok_ref, xbuf.at[y], y_send.at[0], y_recv.at[0], y_dev)
    csend = remote(cache_ref, cbuf.at[y], y_send.at[1], y_recv.at[1], y_dev)
    for copy in wosends + [xsend]:
        copy.start()
    for load in loads[:weight_loads]:
        load.wait()
    k_piece.step(0, (0,))
    qa_piece.step(0)
    qb_piece.step(0)
    csend.start()
    for load in loads[weight_loads:]:
        load.wait()
    k_piece.step(0, (1,))
    for copy in wosends:
        copy.wait_recv()
    s_piece.step(0, (0,))

    row_ids = lax.broadcasted_iota(jnp.int32, (DRAFT, DRAFT), 0)
    col_ids = lax.broadcasted_iota(jnp.int32, (DRAFT, DRAFT), 1)
    eye = (row_ids == col_ids).astype(jnp.float32)
    lane = lax.broadcasted_iota(jnp.int32, (1, HD // 2), 1)
    quarter = HD // 4
    pair = jnp.where(lane < quarter, lane, lane - quarter).astype(jnp.float32)
    freq = jnp.exp(pair * (-2.0 * math.log(10000.0) / (HD // 2)))
    sign = jnp.where(lane < quarter, -1.0, 1.0)
    reaches = []
    positions = []
    for r in range(requests):
        back = (row_ids == parents_ref[r : r + 1, :]).astype(jnp.float32)
        back = jnp.minimum(back + eye, 1.0)
        for sweep in range((DRAFT - 1).bit_length()):
            low = back.astype(jnp.bfloat16)
            back = jnp.minimum(jnp.dot(low, low, preferred_element_type=jnp.float32), 1.0)
        reach = lax.dot_general(
            eye.astype(jnp.bfloat16),
            back.astype(jnp.bfloat16),
            NT,
            preferred_element_type=jnp.float32,
        )
        reach_buf[r] = reach
        depth_buf[r] = jnp.sum(back, axis=0, keepdims=True) - 1.0
        reaches.append(reach)
        depth = jnp.sum(reach, axis=1, keepdims=True) - 1.0
        positions.append(depth + len_ref[r].astype(jnp.float32))
    angle = jnp.concatenate(positions, axis=0) * freq
    cosine = jnp.cos(angle)
    sine = jnp.sin(angle) * sign

    def rotated(value):
        turn = value[:, : HD // 2]
        swapped = jnp.concatenate([turn[:, quarter:], turn[:, :quarter]], axis=1)
        return jnp.concatenate([turn * cosine + swapped * sine, value[:, HD // 2 :]], axis=1)

    xsend.wait_recv()
    wide = jnp.concatenate([xbuf[0], xbuf[1]], axis=1).astype(jnp.float32)
    mean_square = jnp.mean(wide * wide, axis=1, keepdims=True)
    nbuf[...] = (wide * lax.rsqrt(mean_square + 1e-06)).astype(jnp.bfloat16)
    span_rows = level * part_rows

    def project(distance):
        def run(zz):
            for piece in weights:
                piece.gathered(zz)
            source = nbuf[:, pl.ds(pl.multiple_of(zz * span_rows, 128), span_rows)]
            for slot in range(slots + 1):
                at = slice(slot * HD, (slot + 1) * HD)
                block = wbuf[pl.ds(zz * level, level), :, at].reshape(span_rows, HD)
                part = jnp.dot(source, block, preferred_element_type=jnp.float32)
                if distance == 0:
                    accum[:, at] = part
                else:
                    accum[:, at] += part

        each_level(distance, run)

    step(weights, 1)
    relay(weights, 0)
    s_piece.step(0, (1,))
    project(0)
    step(weights, 2)
    relay(weights, 1)
    oa_piece.step(0)
    ob_piece.step(0)
    project(1)
    for distance in range(3, levels):
        step(weights, distance)
        relay(weights, distance - 1)
        if distance == 3:
            step(outputs, 1)
        project(distance - 1)
    relay(outputs, 0)
    relay(weights, levels - 1)
    project(levels - 1)

    projected = accum[:, qcols:]

    @pl.when(y == 0)
    def _():
        kvbuf[0] = rotated(projected).astype(jnp.bfloat16)

    @pl.when(y == 1)
    def _():
        kvbuf[1] = projected.astype(jnp.bfloat16)

    kvsend = remote(kvbuf.at[y], kvbuf.at[y], y_send.at[2], y_recv.at[2], y_dev)
    kvsend.start()
    step(outputs, 2)
    relay(outputs, 1)
    for slot in range(slots):
        value = rotated(accum[:, slot * HD : (slot + 1) * HD])
        qbuf[slot] = (value * HD ** (-0.5)).astype(jnp.bfloat16)
    kvsend.wait_recv()
    csend.wait_recv()

    def attend_one(r):
        span = slice(r * DRAFT, (r + 1) * DRAFT)
        queries = qbuf[:, span, :].reshape(slots * DRAFT, HD)
        ids = [lax.rem(table_ref[r, j], NPR) for j in range(NPR)]
        keys = jnp.concatenate([cbuf[r, i, 0] for i in ids], axis=0)
        values = jnp.concatenate([cbuf[r, i, 1] for i in ids], axis=0)
        span_len = NPR * PAGE
        slot_ids = lax.broadcasted_iota(jnp.int32, (DRAFT, span_len), 1)
        first = positions[r].astype(jnp.int32) - WINDOW
        visible = (slot_ids < len_ref[r]) & (slot_ids > first)
        cache_bias = jnp.where(visible, 0.0, -1e30)
        tree_bias = jnp.where(reaches[r] > 0.5, 0.0, -1e30)
        scores = lax.dot_general(queries, keys, NT, preferred_element_type=jnp.float32)
        tree = lax.dot_general(queries, kvbuf[0, span, :], NT, preferred_element_type=jnp.float32)
        scores = jnp.where(cache_bias[None] < 0.0, -1e30, scores.reshape(slots, DRAFT, span_len))
        tree = jnp.where(tree_bias[None] < 0.0, -1e30, tree.reshape(slots, DRAFT, DRAFT))
        peak = jnp.maximum(
            jnp.max(scores, axis=-1, keepdims=True), jnp.max(tree, axis=-1, keepdims=True)
        )
        scores = jnp.exp(scores - peak)
        tree = jnp.exp(tree - peak)
        total = jnp.sum(scores, axis=-1, keepdims=True) + jnp.sum(tree, axis=-1, keepdims=True)
        scores = (scores / total).astype(jnp.bfloat16).reshape(slots * DRAFT, span_len)
        tree = (tree / total).astype(jnp.bfloat16).reshape(slots * DRAFT, DRAFT)
        result = jnp.dot(scores, values, preferred_element_type=jnp.float32)
        result = result + jnp.dot(tree, kvbuf[1, span, :], preferred_element_type=jnp.float32)
        result = result.astype(jnp.bfloat16)
        for slot in range(slots):
            mixbuf[span, slot * HD : (slot + 1) * HD] = result[slot * DRAFT : (slot + 1) * DRAFT]

    def refresh_one():
        length = len_ref[y]
        own_reach = reach_buf[y]
        on_path = jnp.sum(jnp.where(row_ids == leaf_ref[y], own_reach, 0.0), axis=0, keepdims=True)
        depth_row = depth_buf[y].astype(jnp.int32)
        keep = pl.ds(pl.multiple_of(y * DRAFT, DRAFT), DRAFT)
        new_keys = kvbuf[0, keep, :]
        new_values = kvbuf[1, keep, :]
        slot_ids = lax.broadcasted_iota(jnp.int32, (PAGE, DRAFT), 0)
        for page in range(NPR):
            logical = jnp.int32(0)
            for j in range(1, NPR):
                logical = logical + jnp.where(lax.rem(table_ref[y, j], NPR) == page, j, 0)
            chosen = (on_path > 0.5) & (depth_row == slot_ids + (logical * PAGE - length))
            selector = chosen.astype(jnp.float32)
            written = jnp.sum(selector, axis=1, keepdims=True) > 0.5
            selector = selector.astype(jnp.bfloat16)
            for entry, new in ((0, new_keys), (1, new_values)):
                placed = jnp.dot(selector, new, preferred_element_type=jnp.float32)
                old = cbuf[y, page, entry].astype(jnp.float32)
                cache_out_ref[page, entry] = jnp.where(written, placed, old).astype(jnp.bfloat16)

    width = level * narrow

    def part_copy(zz):
        return remote(psend.at[zz], precv.at[zz], part_send.at[zz], part_recv.at[zz], y_dev)

    def output_level(zz):
        for piece in outputs:
            piece.gathered(zz)
        mixed = mixbuf[...]
        block = obuf[other, pl.ds(zz * level, level)].reshape(width, qcols)
        value = lax.dot_general(mixed, block, NT, preferred_element_type=jnp.float32)
        psend[zz] = value.astype(jnp.bfloat16)
        part_copy(zz).start()
        block = obuf[y, pl.ds(zz * level, level)].reshape(width, qcols)
        value = lax.dot_general(mixed, block, NT, preferred_element_type=jnp.float32)
        pown[zz] = value.astype(jnp.bfloat16)

    attend_one(0)
    for distance in range(3, levels):
        step(outputs, distance)
        relay(outputs, distance - 1)
    for r in range(1, requests):
        attend_one(r)
    for distance in range(levels - 1):
        each_level(distance, output_level)
    refresh_one()
    relay(outputs, levels - 1)
    each_level(levels - 1, output_level)
    sums = []
    for zz in range(levels):
        part_copy(zz).wait_recv()
        sums.append(pown[zz].astype(jnp.float32) + precv[zz].astype(jnp.float32))
    out_ref[...] = jnp.concatenate(sums, axis=1).astype(jnp.bfloat16)
    for piece in weights + outputs:
        piece.drain()
    for copy in [xsend, csend, kvsend] + wosends + [part_copy(zz) for zz in range(levels)]:
        copy.wait_send()


def fused(tokens, query_weight, keyvalue_weight, output_weight, cache, page_table, parents, cache_len, accepted_leaf):
    tok_count = lax.axis_size("tok")
    heads = lax.axis_size("head")
    slots = HQ // heads
    rows, half = tokens.shape
    part_rows = query_weight.shape[0]
    narrow = output_weight.shape[1]
    requests = parents.shape[0]
    pages = cache.shape[0]
    qcols = slots * HD
    positions = tok_count // CORES
    levels = positions // XS
    hbm = pl.BlockSpec(memory_space=pl.ANY)
    vmem = pl.BlockSpec(memory_space=pltpu.VMEM)
    smem = pl.BlockSpec(memory_space=pltpu.SMEM)
    bf16 = jnp.bfloat16
    scratch = [
        pltpu.VMEM((tok_count, part_rows, qcols + HD), bf16),
        pltpu.VMEM((heads, tok_count, narrow, qcols), bf16),
        pltpu.VMEM((heads, rows, half), bf16),
        pltpu.VMEM((heads,) + cache.shape, bf16),
        pltpu.VMEM((2, rows, HD), bf16),
        pltpu.VMEM((slots, rows, HD), bf16),
        pltpu.VMEM((rows, qcols), bf16),
        pltpu.VMEM((requests, DRAFT, DRAFT), jnp.float32),
        pltpu.VMEM((requests, 1, DRAFT), jnp.float32),
        pltpu.VMEM((rows, half * heads), bf16),
        pltpu.VMEM((rows, qcols + HD), jnp.float32),
        pltpu.VMEM((levels, rows, half // levels), bf16),
        pltpu.VMEM((levels, rows, half // levels), bf16),
        pltpu.VMEM((levels, rows, half // levels), bf16),
        pltpu.SemaphoreType.DMA((3 + slots,)),
        pltpu.SemaphoreType.DMA((3 + slots,)),
        pltpu.SemaphoreType.DMA((levels,)),
        pltpu.SemaphoreType.DMA((levels,)),
        pltpu.SemaphoreType.DMA((2 * slots + 3,)),
    ]
    for piece in range(6):
        scratch += [pltpu.SemaphoreType.DMA((positions,))] * 4
        scratch += [pltpu.SemaphoreType.DMA((tok_count,))]
    return pl.pallas_call(
        fused_kernel,
        out_shape=(
            jax.ShapeDtypeStruct(tokens.shape, bf16),
            jax.ShapeDtypeStruct(cache.shape, bf16),
        ),
        in_specs=[hbm] * 5 + [vmem] + [smem] * 3,
        out_specs=(vmem, vmem),
        scratch_shapes=scratch,
        compiler_params=pltpu.CompilerParams(
            collective_id=0, has_side_effects=True, vmem_limit_bytes=48 * 1024 * 1024
        ),
        cost_estimate=pl.CostEstimate(
            flops=4 * rows * HD * HQ * HD * 5, bytes_accessed=1 << 22, transcendentals=1 << 19
        ),
    )(
        tokens,
        query_weight,
        keyvalue_weight,
        jnp.transpose(output_weight),
        cache,
        parents,
        page_table,
        cache_len,
        accepted_leaf,
    )


def fits(tok_count, head_count, args):
    tokens, query_weight, _, output_weight, cache, _, parents, _, _ = args
    return (
        head_count == 2
        and tok_count % (2 * XS * CORES) == 0
        and tok_count >= 3 * XS * CORES
        and query_weight.shape[0] % TILE == 0
        and output_weight.shape[1] % TILE == 0
        and output_weight.shape[1] >= 3 * TILE
        and XS * CORES * query_weight.shape[0] % 128 == 0
        and cache.shape[0] == NPR
        and parents.shape[0] == head_count
    )


def dispatch(*args):
    if fits(lax.axis_size("tok"), lax.axis_size("head"), args):
        return fused(*args)
    return shards(*args)


def solution(mesh):
    in_specs = (
        P("tok", "head"),
        P("tok", None),
        P("tok", None),
        P(None, ("head", "tok")),
        P(("tok", "head"), None, None, None),
        P("tok", None),
        P("tok", None),
        P("tok"),
        P("tok"),
    )
    out_specs = (P("tok", "head"), P(("tok", "head"), None, None, None))
    return jax.shard_map(
        dispatch, mesh=mesh, in_specs=in_specs, out_specs=out_specs, check_vma=False
    )
```

```python
import math

import jax
import jax.numpy as jnp
from jax import lax
from jax.experimental import pallas as pl
from jax.experimental.pallas import tpu as pltpu
from jax.sharding import PartitionSpec as P

HQ = 10
HD = 256
DRAFT = 64
PAGE = 128
NPR = 4
WINDOW = 256
CORES = 2
XS = 2
TILE = 16
MESH = pl.DeviceIdType.MESH
NT = (((1,), (1,)), ((), ()))


def ancestry(parent_row):
    node_ids = jnp.arange(DRAFT, dtype=jnp.int32)
    link = (parent_row[:, None] == node_ids[None, :]).astype(jnp.float32)
    reach = jnp.minimum(link + jnp.eye(DRAFT, dtype=jnp.float32), 1.0)
    for sweep in range((DRAFT - 1).bit_length()):
        reach = jnp.minimum(jnp.dot(reach, reach, precision=lax.Precision.HIGHEST), 1.0)
    depth = (jnp.sum(reach, axis=1) - 1.0).astype(jnp.int32)
    return (reach, depth)


def rotate(values, position):
    half = HD // 4
    freq = jnp.exp(jnp.arange(half, dtype=jnp.float32) * (-2.0 * math.log(10000.0) / (HD // 2)))
    angle = position.astype(jnp.float32)[..., None] * freq
    cosine = jnp.cos(angle)
    sine = jnp.sin(angle)
    first = values[..., :half]
    second = values[..., half : 2 * half]
    return jnp.concatenate(
        [first * cosine - second * sine, second * cosine + first * sine, values[..., 2 * half :]],
        axis=-1,
    )


def attend(queries, cache_keys, cache_values, tree_keys, tree_values, lengths, position, reach):
    window_span = cache_keys.shape[1]
    slot_ids = jnp.arange(window_span, dtype=jnp.int32)
    visible = (slot_ids[None, None, :] < lengths[:, None, None]) & (
        slot_ids[None, None, :] > position[:, :, None] - WINDOW
    )
    cache_scores = jnp.einsum(
        "rnhd,rcd->rhnc", queries, cache_keys, preferred_element_type=jnp.float32
    )
    tree_scores = jnp.einsum(
        "rnhd,rmd->rhnm", queries, tree_keys, preferred_element_type=jnp.float32
    )
    cache_scores = jnp.where(visible[:, None], cache_scores, -1e30)
    tree_scores = jnp.where(reach[:, None] > 0.5, tree_scores, -1e30)
    row_peak = jnp.maximum(jnp.max(cache_scores, axis=-1), jnp.max(tree_scores, axis=-1))[..., None]
    cache_weights = jnp.exp(cache_scores - row_peak)
    tree_weights = jnp.exp(tree_scores - row_peak)
    denominator = jnp.sum(cache_weights, axis=-1, keepdims=True) + jnp.sum(
        tree_weights, axis=-1, keepdims=True
    )
    cache_weights = (cache_weights / denominator).astype(jnp.bfloat16)
    tree_weights = (tree_weights / denominator).astype(jnp.bfloat16)
    result = jnp.einsum(
        "rhnc,rcd->rnhd", cache_weights, cache_values, preferred_element_type=jnp.float32
    )
    result = result + jnp.einsum(
        "rhnm,rmd->rnhd", tree_weights, tree_values, preferred_element_type=jnp.float32
    )
    return result.astype(jnp.bfloat16)


def refresh(logical_pages, length, leaf, reach, depth, new_keys, new_values):
    count = logical_pages.shape[0] * logical_pages.shape[2]
    logical = jnp.transpose(logical_pages, (1, 0, 2, 3)).reshape(2, count, HD)
    slot_ids = jnp.arange(count, dtype=jnp.int32)
    on_path = reach[leaf]
    selector = ((on_path[None, :] > 0.5) & (depth[None, :] == slot_ids[:, None] - length)).astype(
        jnp.float32
    )
    placed_keys = jnp.dot(selector, new_keys.astype(jnp.float32), precision=lax.Precision.HIGHEST)
    placed_values = jnp.dot(
        selector, new_values.astype(jnp.float32), precision=lax.Precision.HIGHEST
    )
    placed = jnp.stack([placed_keys, placed_values]).astype(jnp.bfloat16)
    written = jnp.sum(selector, axis=1) > 0.5
    logical = jnp.where(written[None, :, None], placed, logical)
    return jnp.transpose(
        logical.reshape(2, logical_pages.shape[0], logical_pages.shape[2], HD), (1, 0, 2, 3)
    )


def contract(source, piece):
    return jnp.dot(source, piece, preferred_element_type=jnp.float32)


def project_memory(rows, keyvalue_weight, position):
    projected = contract(rows, lax.all_gather(keyvalue_weight, "tok", axis=0, tiled=True))
    new_keys = rotate(projected[:, :HD], position).astype(jnp.bfloat16)
    new_values = projected[:, HD:].astype(jnp.bfloat16)
    return (new_keys, new_values)


def split_pages(page_blocks, count):
    cache_keys = page_blocks[:, :, 0].reshape(count, NPR * PAGE, HD)
    cache_values = page_blocks[:, :, 1].reshape(count, NPR * PAGE, HD)
    return (cache_keys, cache_values)


def reduce_heads(mixed, output_weight, safe_heads, head_mask, slots_per):
    head_count = lax.axis_size("head")
    tok_count = lax.axis_size("tok")
    narrow = output_weight.shape[1]
    blocks = lax.all_gather(output_weight, "head", axis=1, tiled=True)
    part_cols = blocks.shape[1]
    my_output_weight = (
        jnp.take(blocks.reshape(HQ, HD, part_cols), safe_heads, axis=0) * head_mask[:, None, None]
    )
    my_output_weight = my_output_weight.reshape(slots_per * HD, part_cols)
    partial_value = jnp.dot(
        mixed,
        lax.all_gather(my_output_weight, "tok", axis=1, tiled=True),
        preferred_element_type=jnp.float32,
    ).astype(jnp.bfloat16)
    row_count = partial_value.shape[0]
    partial_value = partial_value.reshape(row_count, tok_count, head_count, narrow)
    partial_value = jnp.transpose(partial_value, (0, 2, 1, 3)).reshape(
        row_count, tok_count * head_count * narrow
    )
    partial_value = lax.optimization_barrier(partial_value)
    summed = lax.psum_scatter(
        partial_value.astype(jnp.float32).astype(jnp.bfloat16),
        "head",
        scatter_dimension=1,
        tiled=True,
    )
    return summed


def shards(
    tokens,
    query_weight,
    keyvalue_weight,
    output_weight,
    cache,
    page_table,
    parents,
    cache_len,
    accepted_leaf,
):
    head_count = lax.axis_size("head")
    head_index = lax.axis_index("head")
    tok_index = lax.axis_index("tok")
    slots_per = -(-HQ // head_count)
    requests = parents.shape[0]
    owned = requests // head_count
    rows_owned = owned * DRAFT
    pages_dev = cache.shape[0]
    gathered = lax.all_gather(tokens, "head", axis=1, tiled=True)
    wide = gathered.astype(jnp.float32)
    mean_square = jnp.mean(wide * wide, axis=1, keepdims=True)
    normed = (wide * lax.rsqrt(mean_square + 1e-06)).astype(jnp.bfloat16)
    reach, depth = jax.vmap(ancestry)(parents)
    position = cache_len[:, None] + depth
    flat_pos = position.reshape(-1)
    head_ids = head_index + head_count * jnp.arange(slots_per, dtype=jnp.int32)
    usable = head_ids < HQ
    safe_heads = jnp.minimum(head_ids, HQ - 1)
    head_mask = usable.astype(jnp.bfloat16)
    part_rows = query_weight.shape[0]
    my_query_weight = (
        jnp.take(query_weight.reshape(part_rows, HQ, HD), safe_heads, axis=1)
        * head_mask[None, :, None]
    )
    my_query_weight = my_query_weight.reshape(part_rows, slots_per * HD)
    queries = contract(normed, lax.all_gather(my_query_weight, "tok", axis=0, tiled=True))
    queries = (rotate(queries.reshape(-1, slots_per, HD), flat_pos[:, None]) * HD ** (-0.5)).astype(
        jnp.bfloat16
    )
    own_start = head_index * rows_owned
    own_reach = lax.dynamic_slice_in_dim(reach, head_index * owned, owned, 0)
    own_depth = lax.dynamic_slice_in_dim(depth, head_index * owned, owned, 0)
    own_len = lax.dynamic_slice_in_dim(cache_len, head_index * owned, owned, 0)
    own_leaf = lax.dynamic_slice_in_dim(accepted_leaf, head_index * owned, owned, 0)
    device = tok_index * head_count + head_index
    own_table = (
        lax.dynamic_slice_in_dim(page_table, head_index * owned, owned, 0) - device * pages_dev
    )
    own_pages = jnp.take(cache, own_table.reshape(-1), axis=0).reshape(owned, NPR, 2, PAGE, HD)
    tree_keys, tree_values = project_memory(normed, keyvalue_weight, flat_pos)
    own_keys = lax.dynamic_slice_in_dim(tree_keys, own_start, rows_owned, 0)
    own_values = lax.dynamic_slice_in_dim(tree_values, own_start, rows_owned, 0)
    page_pool = lax.all_gather(cache, "head", axis=0, tiled=True)
    local_ids = page_table - tok_index * head_count * pages_dev
    page_blocks = jnp.take(page_pool, local_ids.reshape(-1), axis=0).reshape(
        requests, NPR, 2, PAGE, HD
    )
    cache_keys, cache_values = split_pages(page_blocks, requests)
    result = attend(
        queries.reshape(requests, DRAFT, slots_per, HD),
        cache_keys,
        cache_values,
        tree_keys.reshape(requests, DRAFT, HD),
        tree_values.reshape(requests, DRAFT, HD),
        cache_len,
        position,
        reach,
    )
    mixed = result.reshape(-1, slots_per * HD)
    attended = reduce_heads(mixed, output_weight, safe_heads, head_mask, slots_per)
    new_pages = jax.vmap(refresh)(
        own_pages,
        own_len,
        own_leaf,
        own_reach,
        own_depth,
        own_keys.reshape(owned, DRAFT, HD),
        own_values.reshape(owned, DRAFT, HD),
    )
    flat_ids = own_table.reshape(-1)
    matches = (flat_ids[:, None] == jnp.arange(pages_dev, dtype=jnp.int32)[None, :]).astype(
        jnp.int32
    )
    inverse = jnp.sum(matches * jnp.arange(pages_dev, dtype=jnp.int32)[:, None], axis=0)
    cache_out = jnp.take(new_pages.reshape(pages_dev, 2, PAGE, HD), inverse, axis=0)
    return (attended, cache_out)


def fused_kernel(
    tok_ref,
    qw_ref,
    kvw_ref,
    wo_ref,
    cache_ref,
    parents_ref,
    table_ref,
    len_ref,
    leaf_ref,
    out_ref,
    cache_out_ref,
    wbuf,
    obuf,
    xbuf,
    cbuf,
    kvbuf,
    qbuf,
    mixbuf,
    reach_buf,
    depth_buf,
    nbuf,
    accum,
    psend,
    pown,
    precv,
    fsend,
    final,
    y_send,
    y_recv,
    part_send,
    part_recv,
    final_send,
    final_recv,
    mix_send,
    mix_recv,
    load_sem,
    *piece_sems,
):
    tok_count = wbuf.shape[0]
    levels = tok_count // (XS * CORES)
    slots = qbuf.shape[0]
    rows = tok_ref.shape[0]
    narrow = wo_ref.shape[0]
    requests = parents_ref.shape[0]
    level = XS * CORES
    part_rows = wbuf.shape[1]
    qcols = slots * HD
    me = lax.axis_index("tok")
    y = lax.axis_index("head")
    other = 1 - y
    core = lax.rem(me, CORES)
    xpos = lax.rem(lax.div(me, CORES), XS)
    z = lax.div(me, CORES * XS)

    def tok_at(zz, xx, cc):
        return (zz * XS + xx) * CORES + cc

    up_dev = (jnp.minimum(me + XS * CORES, tok_count - 1), y)
    down_dev = (jnp.maximum(me - XS * CORES, 0), y)
    x_dev = (tok_at(z, 1 - xpos, core), y)
    core_dev = (tok_at(z, xpos, 1 - core), y)
    y_dev = (me, other)
    has_up = z < levels - 1
    has_down = z > 0

    def columns(slot, group):
        return pl.ds(pl.multiple_of((2 * slot + group) * HD, HD), HD)

    loads = [
        (
            qw_ref.at[:, columns(slot, y)],
            wbuf.at[me, :, slot * HD : (slot + 1) * HD],
        )
        for slot in range(slots)
    ]
    loads.append((kvw_ref.at[:, pl.ds(pl.multiple_of(y * HD, HD), HD)], wbuf.at[me, :, qcols:]))
    weight_loads = len(loads)
    loads += [
        (
            wo_ref.at[:, columns(slot, y)],
            obuf.at[y, me, :, slot * HD : (slot + 1) * HD],
        )
        for slot in range(slots)
    ]
    loads += [(tok_ref, xbuf.at[y]), (cache_ref, cbuf.at[y])]
    loads = [
        pltpu.make_async_copy(source, target, load_sem.at[index])
        for index, (source, target) in enumerate(loads)
    ]
    for load in loads:
        load.start()

    barrier = pltpu.get_barrier_semaphore()
    for device in (x_dev, core_dev, y_dev):
        pl.semaphore_signal(barrier, inc=1, device_id=device, device_id_type=MESH)

    @pl.when(has_up)
    def _():
        pl.semaphore_signal(barrier, inc=1, device_id=up_dev, device_id_type=MESH)

    @pl.when(has_down)
    def _():
        pl.semaphore_signal(barrier, inc=1, device_id=down_dev, device_id_type=MESH)

    pl.semaphore_wait(barrier, 3 + has_up.astype(jnp.int32) + has_down.astype(jnp.int32))

    def remote(source, target, send_sem, recv_sem, device):
        return pltpu.make_async_remote_copy(
            src_ref=source,
            dst_ref=target,
            send_sem=send_sem,
            recv_sem=recv_sem,
            device_id=device,
            device_id_type=MESH,
        )

    def each_level(distance, run):
        if distance == 0:
            run(z)
            return
        pl.when(z - distance >= 0)(lambda: run(z - distance))
        pl.when(z + distance < levels)(lambda: run(z + distance))

    class Piece:
        def __init__(self, view, sems, cross_x):
            self.view = view
            self.up, self.down, self.xs, self.cs, self.recv = sems
            self.cross_x = cross_x

        def copy(self, t, sems, device):
            ref = self.view(t)
            return remote(ref, ref, sems.at[lax.div(t, CORES)], self.recv.at[t], device)

        def along(self, t, act, up, down):
            if up:
                pl.when(has_up)(lambda: act(self.copy(t, self.up, up_dev)))
            if down:
                pl.when(has_down)(lambda: act(self.copy(t, self.down, down_dev)))

        def spread(self, t, own_x, act):
            if own_x and self.cross_x:
                act(self.copy(t, self.xs, x_dev))
            act(self.copy(t, self.cs, core_dev))

        def arrive(self, t):
            self.copy(t, self.cs, core_dev).wait_recv()

        def visit(self, distance, sending, act):
            def go(zz, up, down):
                t = tok_at(zz, xpos, core)
                if sending and distance:
                    self.arrive(t)
                self.along(t, act, up, down)
                self.spread(t, True, act)

            if distance == 0:
                go(z, True, True)
                return
            pl.when(z - distance >= 0)(lambda: go(z - distance, True, False))
            pl.when(z + distance < levels)(lambda: go(z + distance, False, True))

        def cross(self, distance, sending, act):
            if not self.cross_x:
                return

            def go(zz):
                t = tok_at(zz, 1 - xpos, core)
                if sending:
                    self.arrive(t)
                self.spread(t, False, act)

            each_level(distance, go)

        def step(self, distance):
            self.visit(distance, True, lambda copy: copy.start())

        def relay(self, distance):
            self.cross(distance, True, lambda copy: copy.start())

        def gathered(self, zz):
            self.arrive(tok_at(zz, xpos, 1 - core))
            if self.cross_x:
                self.arrive(tok_at(zz, 1 - xpos, 1 - core))

        def drain(self):
            for distance in range(levels):
                self.visit(distance, False, lambda copy: copy.wait_send())
                self.cross(distance, False, lambda copy: copy.wait_send())

    pieces = [piece_sems[5 * i : 5 * i + 5] for i in range(4)]
    cut = (slots + 1) // 2 * HD
    mid = (narrow // 2 + TILE - 1) // TILE * TILE
    weights = (
        Piece(lambda t: wbuf.at[t, :, :cut], pieces[0], True),
        Piece(lambda t: wbuf.at[t, :, cut:], pieces[1], True),
    )
    outputs = (
        Piece(lambda t: obuf.at[:, t, :mid], pieces[2], False),
        Piece(lambda t: obuf.at[:, t, mid:], pieces[3], False),
    )

    def step(group, distance):
        for piece in group:
            piece.step(distance)

    def relay(group, distance):
        for piece in group:
            piece.relay(distance)

    wosends = [
        remote(
            wo_ref.at[:, columns(slot, other)],
            obuf.at[y, me, :, slot * HD : (slot + 1) * HD],
            y_send.at[3 + slot],
            y_recv.at[3 + slot],
            y_dev,
        )
        for slot in range(slots)
    ]
    xsend = remote(tok_ref, xbuf.at[y], y_send.at[0], y_recv.at[0], y_dev)
    csend = remote(cache_ref, cbuf.at[y], y_send.at[1], y_recv.at[1], y_dev)
    for copy in wosends + [xsend]:
        copy.start()
    for load in loads[:weight_loads]:
        load.wait()
    step(weights, 0)
    csend.start()
    for load in loads[weight_loads:]:
        load.wait()

    row_ids = lax.broadcasted_iota(jnp.int32, (DRAFT, DRAFT), 0)
    col_ids = lax.broadcasted_iota(jnp.int32, (DRAFT, DRAFT), 1)
    eye = (row_ids == col_ids).astype(jnp.float32)
    lane = lax.broadcasted_iota(jnp.int32, (1, HD // 2), 1)
    quarter = HD // 4
    pair = jnp.where(lane < quarter, lane, lane - quarter).astype(jnp.float32)
    freq = jnp.exp(pair * (-2.0 * math.log(10000.0) / (HD // 2)))
    sign = jnp.where(lane < quarter, -1.0, 1.0)
    reaches = []
    positions = []
    for r in range(requests):
        back = (row_ids == parents_ref[r : r + 1, :]).astype(jnp.float32)
        back = jnp.minimum(back + eye, 1.0)
        for sweep in range((DRAFT - 1).bit_length()):
            low = back.astype(jnp.bfloat16)
            back = jnp.minimum(jnp.dot(low, low, preferred_element_type=jnp.float32), 1.0)
        reach = lax.dot_general(
            eye.astype(jnp.bfloat16),
            back.astype(jnp.bfloat16),
            NT,
            preferred_element_type=jnp.float32,
        )
        reach_buf[r] = reach
        depth_buf[r] = jnp.sum(back, axis=0, keepdims=True) - 1.0
        reaches.append(reach)
        depth = jnp.sum(reach, axis=1, keepdims=True) - 1.0
        positions.append(depth + len_ref[r].astype(jnp.float32))
    angle = jnp.concatenate(positions, axis=0) * freq
    cosine = jnp.cos(angle)
    sine = jnp.sin(angle) * sign

    def rotated(value):
        turn = value[:, : HD // 2]
        swapped = jnp.concatenate([turn[:, quarter:], turn[:, :quarter]], axis=1)
        return jnp.concatenate([turn * cosine + swapped * sine, value[:, HD // 2 :]], axis=1)

    xsend.wait_recv()
    wide = jnp.concatenate([xbuf[0], xbuf[1]], axis=1).astype(jnp.float32)
    mean_square = jnp.mean(wide * wide, axis=1, keepdims=True)
    nbuf[...] = (wide * lax.rsqrt(mean_square + 1e-06)).astype(jnp.bfloat16)
    span_rows = level * part_rows

    def project(distance):
        def run(zz):
            for piece in weights:
                piece.gathered(zz)
            source = nbuf[:, pl.ds(pl.multiple_of(zz * span_rows, 128), span_rows)]
            for slot in range(slots + 1):
                at = slice(slot * HD, (slot + 1) * HD)
                block = wbuf[pl.ds(zz * level, level), :, at].reshape(span_rows, HD)
                part = jnp.dot(source, block, preferred_element_type=jnp.float32)
                if distance == 0:
                    accum[:, at] = part
                else:
                    accum[:, at] += part

        each_level(distance, run)

    step(weights, 1)
    relay(weights, 0)
    project(0)
    step(weights, 2)
    relay(weights, 1)
    for copy in wosends:
        copy.wait_recv()
    step(outputs, 0)
    project(1)
    for distance in range(3, levels):
        step(weights, distance)
        relay(weights, distance - 1)
        if distance == 3:
            step(outputs, 1)
        project(distance - 1)
    relay(weights, levels - 1)
    project(levels - 1)

    projected = accum[:, qcols:]

    @pl.when(y == 0)
    def _():
        kvbuf[0] = rotated(projected).astype(jnp.bfloat16)

    @pl.when(y == 1)
    def _():
        kvbuf[1] = projected.astype(jnp.bfloat16)

    kvsend = remote(kvbuf.at[y], kvbuf.at[y], y_send.at[2], y_recv.at[2], y_dev)
    kvsend.start()
    step(outputs, 2)
    for slot in range(slots):
        value = rotated(accum[:, slot * HD : (slot + 1) * HD])
        qbuf[slot] = (value * HD ** (-0.5)).astype(jnp.bfloat16)
    kvsend.wait_recv()
    csend.wait_recv()

    def attend_one(r):
        span = slice(r * DRAFT, (r + 1) * DRAFT)
        queries = qbuf[:, span, :].reshape(slots * DRAFT, HD)
        ids = [lax.rem(table_ref[r, j], NPR) for j in range(NPR)]
        keys = jnp.concatenate([cbuf[r, i, 0] for i in ids], axis=0)
        values = jnp.concatenate([cbuf[r, i, 1] for i in ids], axis=0)
        span_len = NPR * PAGE
        slot_ids = lax.broadcasted_iota(jnp.int32, (DRAFT, span_len), 1)
        first = positions[r].astype(jnp.int32) - WINDOW
        visible = (slot_ids < len_ref[r]) & (slot_ids > first)
        cache_bias = jnp.where(visible, 0.0, -1e30)
        tree_bias = jnp.where(reaches[r] > 0.5, 0.0, -1e30)
        scores = lax.dot_general(queries, keys, NT, preferred_element_type=jnp.float32)
        tree = lax.dot_general(queries, kvbuf[0, span, :], NT, preferred_element_type=jnp.float32)
        scores = jnp.where(cache_bias[None] < 0.0, -1e30, scores.reshape(slots, DRAFT, span_len))
        tree = jnp.where(tree_bias[None] < 0.0, -1e30, tree.reshape(slots, DRAFT, DRAFT))
        peak = jnp.maximum(
            jnp.max(scores, axis=-1, keepdims=True), jnp.max(tree, axis=-1, keepdims=True)
        )
        scores = jnp.exp(scores - peak)
        tree = jnp.exp(tree - peak)
        total = jnp.sum(scores, axis=-1, keepdims=True) + jnp.sum(tree, axis=-1, keepdims=True)
        scores = (scores / total).astype(jnp.bfloat16).reshape(slots * DRAFT, span_len)
        tree = (tree / total).astype(jnp.bfloat16).reshape(slots * DRAFT, DRAFT)
        result = jnp.dot(scores, values, preferred_element_type=jnp.float32)
        result = result + jnp.dot(tree, kvbuf[1, span, :], preferred_element_type=jnp.float32)
        result = result.astype(jnp.bfloat16)
        for slot in range(slots):
            mixbuf[xpos, span, slot * HD : (slot + 1) * HD] = result[slot * DRAFT : (slot + 1) * DRAFT]

    def refresh_one():
        length = len_ref[y]
        own_reach = reach_buf[y]
        on_path = jnp.sum(jnp.where(row_ids == leaf_ref[y], own_reach, 0.0), axis=0, keepdims=True)
        depth_row = depth_buf[y].astype(jnp.int32)
        keep = pl.ds(pl.multiple_of(y * DRAFT, DRAFT), DRAFT)
        new_keys = kvbuf[0, keep, :]
        new_values = kvbuf[1, keep, :]
        slot_ids = lax.broadcasted_iota(jnp.int32, (PAGE, DRAFT), 0)
        for page in range(NPR):
            logical = jnp.int32(0)
            for j in range(1, NPR):
                logical = logical + jnp.where(lax.rem(table_ref[y, j], NPR) == page, j, 0)
            chosen = (on_path > 0.5) & (depth_row == slot_ids + (logical * PAGE - length))
            selector = chosen.astype(jnp.float32)
            written = jnp.sum(selector, axis=1, keepdims=True) > 0.5
            selector = selector.astype(jnp.bfloat16)
            for entry, new in ((0, new_keys), (1, new_values)):
                placed = jnp.dot(selector, new, preferred_element_type=jnp.float32)
                old = cbuf[y, page, entry].astype(jnp.float32)
                cache_out_ref[page, entry] = jnp.where(written, placed, old).astype(jnp.bfloat16)

    width = CORES * narrow

    def part_copy(zz):
        return remote(psend.at[zz], precv.at[zz], part_send.at[zz], part_recv.at[zz], y_dev)

    def final_copy(zz):
        ref = final.at[xpos, zz]
        return remote(fsend.at[zz], ref, final_send.at[zz], final_recv.at[zz], x_dev)

    def mix_copy(r):
        ref = mixbuf.at[xpos, r * DRAFT : (r + 1) * DRAFT]
        return remote(ref, ref, mix_send.at[r], mix_recv.at[r], x_dev)

    def output_level(zz):
        for piece in outputs:
            piece.gathered(zz)
        mixed = mixbuf[...].reshape(XS * rows, qcols)
        own = pl.ds(zz * level + xpos * CORES, CORES)
        block = obuf[other, own].reshape(width, qcols)
        value = lax.dot_general(mixed, block, NT, preferred_element_type=jnp.float32)
        psend[zz] = value.astype(jnp.bfloat16).reshape(XS, rows, width)
        part_copy(zz).start()
        block = obuf[y, own].reshape(width, qcols)
        value = lax.dot_general(mixed, block, NT, preferred_element_type=jnp.float32)
        pown[zz] = value.astype(jnp.bfloat16).reshape(XS, rows, width)

    def sum_level(zz):
        part_copy(zz).wait_recv()

        def summed(xx):
            total = pown[zz, xx].astype(jnp.float32) + precv[zz, xx].astype(jnp.float32)
            return total.astype(jnp.bfloat16)

        fsend[zz] = summed(1 - xpos)
        final_copy(zz).start()
        final[xpos, zz] = summed(xpos)

    attend_one(0)
    mix_copy(0).start()
    for distance in range(3, levels):
        step(outputs, distance)
    for r in range(1, requests):
        attend_one(r)
        mix_copy(r).start()
    refresh_one()
    for r in range(requests):
        mix_copy(r).wait_recv()
    for distance in range(levels):
        each_level(distance, output_level)
        if distance > 0:
            each_level(distance - 1, sum_level)
    each_level(levels - 1, sum_level)
    for zz in range(levels):
        final_copy(zz).wait_recv()
    done = [final[xx, zz] for zz in range(levels) for xx in range(XS)]
    out_ref[...] = jnp.concatenate(done, axis=1)
    for piece in weights + outputs:
        piece.drain()
    for copy in [xsend, csend, kvsend] + wosends + [mix_copy(r) for r in range(requests)]:
        copy.wait_send()
    for zz in range(levels):
        part_copy(zz).wait_send()
        final_copy(zz).wait_send()


def fused(tokens, query_weight, keyvalue_weight, output_weight, cache, page_table, parents, cache_len, accepted_leaf):
    tok_count = lax.axis_size("tok")
    heads = lax.axis_size("head")
    slots = HQ // heads
    rows, half = tokens.shape
    part_rows = query_weight.shape[0]
    narrow = output_weight.shape[1]
    requests = parents.shape[0]
    pages = cache.shape[0]
    qcols = slots * HD
    positions = tok_count // CORES
    levels = positions // XS
    hbm = pl.BlockSpec(memory_space=pltpu.HBM)
    vmem = pl.BlockSpec(memory_space=pltpu.VMEM)
    smem = pl.BlockSpec(memory_space=pltpu.SMEM)
    bf16 = jnp.bfloat16
    scratch = [
        pltpu.VMEM((tok_count, part_rows, qcols + HD), bf16),
        pltpu.VMEM((heads, tok_count, narrow, qcols), bf16),
        pltpu.VMEM((heads, rows, half), bf16),
        pltpu.VMEM((heads,) + cache.shape, bf16),
        pltpu.VMEM((2, rows, HD), bf16),
        pltpu.VMEM((slots, rows, HD), bf16),
        pltpu.VMEM((XS, rows, qcols), bf16),
        pltpu.VMEM((requests, DRAFT, DRAFT), jnp.float32),
        pltpu.VMEM((requests, 1, DRAFT), jnp.float32),
        pltpu.VMEM((rows, half * heads), bf16),
        pltpu.VMEM((rows, qcols + HD), jnp.float32),
        pltpu.VMEM((levels, XS, rows, CORES * narrow), bf16),
        pltpu.VMEM((levels, XS, rows, CORES * narrow), bf16),
        pltpu.VMEM((levels, XS, rows, CORES * narrow), bf16),
        pltpu.VMEM((levels, rows, CORES * narrow), bf16),
        pltpu.VMEM((XS, levels, rows, CORES * narrow), bf16),
        pltpu.SemaphoreType.DMA((3 + slots,)),
        pltpu.SemaphoreType.DMA((3 + slots,)),
        pltpu.SemaphoreType.DMA((levels,)),
        pltpu.SemaphoreType.DMA((levels,)),
        pltpu.SemaphoreType.DMA((levels,)),
        pltpu.SemaphoreType.DMA((levels,)),
        pltpu.SemaphoreType.DMA((requests,)),
        pltpu.SemaphoreType.DMA((requests,)),
        pltpu.SemaphoreType.DMA((2 * slots + 3,)),
    ]
    for piece in range(4):
        scratch += [pltpu.SemaphoreType.DMA((positions,))] * 4
        scratch += [pltpu.SemaphoreType.DMA((tok_count,))]
    return pl.pallas_call(
        fused_kernel,
        out_shape=(
            jax.ShapeDtypeStruct(tokens.shape, bf16),
            jax.ShapeDtypeStruct(cache.shape, bf16),
        ),
        in_specs=[hbm] * 5 + [vmem] + [smem] * 3,
        out_specs=(vmem, vmem),
        scratch_shapes=scratch,
        compiler_params=pltpu.CompilerParams(
            collective_id=0, has_side_effects=True, vmem_limit_bytes=64 * 1024 * 1024
        ),
        cost_estimate=pl.CostEstimate(
            flops=4 * rows * HD * HQ * HD * 5, bytes_accessed=1 << 22, transcendentals=1 << 19
        ),
    )(
        tokens,
        query_weight,
        keyvalue_weight,
        jnp.transpose(output_weight),
        cache,
        parents,
        page_table,
        cache_len,
        accepted_leaf,
    )


def fits(tok_count, head_count, args):
    tokens, query_weight, _, output_weight, cache, _, parents, _, _ = args
    return (
        head_count == 2
        and tok_count % (2 * XS * CORES) == 0
        and tok_count >= 3 * XS * CORES
        and query_weight.shape[0] % TILE == 0
        and output_weight.shape[1] % TILE == 0
        and output_weight.shape[1] >= 3 * TILE
        and XS * CORES * query_weight.shape[0] % 128 == 0
        and cache.shape[0] == NPR
        and parents.shape[0] == head_count
    )


def dispatch(*args):
    if fits(lax.axis_size("tok"), lax.axis_size("head"), args):
        return fused(*args)
    return shards(*args)


def solution(mesh):
    in_specs = (
        P("tok", "head"),
        P("tok", None),
        P("tok", None),
        P(None, ("head", "tok")),
        P(("tok", "head"), None, None, None),
        P("tok", None),
        P("tok", None),
        P("tok"),
        P("tok"),
    )
    out_specs = (P("tok", "head"), P(("tok", "head"), None, None, None))
    return jax.shard_map(
        dispatch, mesh=mesh, in_specs=in_specs, out_specs=out_specs, check_vma=False
    )
```

```python
import math

import jax
import jax.numpy as jnp
from jax import lax
from jax.experimental import pallas as pl
from jax.experimental.pallas import tpu as pltpu
from jax.sharding import PartitionSpec as P

HQ = 10
HD = 256
DRAFT = 64
PAGE = 128
NPR = 4
WINDOW = 256
CORES = 2
XS = 2
TILE = 16
MESH = pl.DeviceIdType.MESH
NT = (((1,), (1,)), ((), ()))


def ancestry(parent_row):
    node_ids = jnp.arange(DRAFT, dtype=jnp.int32)
    link = (parent_row[:, None] == node_ids[None, :]).astype(jnp.float32)
    reach = jnp.minimum(link + jnp.eye(DRAFT, dtype=jnp.float32), 1.0)
    for sweep in range((DRAFT - 1).bit_length()):
        reach = jnp.minimum(jnp.dot(reach, reach, precision=lax.Precision.HIGHEST), 1.0)
    depth = (jnp.sum(reach, axis=1) - 1.0).astype(jnp.int32)
    return (reach, depth)


def rotate(values, position):
    half = HD // 4
    freq = jnp.exp(jnp.arange(half, dtype=jnp.float32) * (-2.0 * math.log(10000.0) / (HD // 2)))
    angle = position.astype(jnp.float32)[..., None] * freq
    cosine = jnp.cos(angle)
    sine = jnp.sin(angle)
    first = values[..., :half]
    second = values[..., half : 2 * half]
    return jnp.concatenate(
        [first * cosine - second * sine, second * cosine + first * sine, values[..., 2 * half :]],
        axis=-1,
    )


def attend(queries, cache_keys, cache_values, tree_keys, tree_values, lengths, position, reach):
    window_span = cache_keys.shape[1]
    slot_ids = jnp.arange(window_span, dtype=jnp.int32)
    visible = (slot_ids[None, None, :] < lengths[:, None, None]) & (
        slot_ids[None, None, :] > position[:, :, None] - WINDOW
    )
    cache_scores = jnp.einsum(
        "rnhd,rcd->rhnc", queries, cache_keys, preferred_element_type=jnp.float32
    )
    tree_scores = jnp.einsum(
        "rnhd,rmd->rhnm", queries, tree_keys, preferred_element_type=jnp.float32
    )
    cache_scores = jnp.where(visible[:, None], cache_scores, -1e30)
    tree_scores = jnp.where(reach[:, None] > 0.5, tree_scores, -1e30)
    row_peak = jnp.maximum(jnp.max(cache_scores, axis=-1), jnp.max(tree_scores, axis=-1))[..., None]
    cache_weights = jnp.exp(cache_scores - row_peak)
    tree_weights = jnp.exp(tree_scores - row_peak)
    denominator = jnp.sum(cache_weights, axis=-1, keepdims=True) + jnp.sum(
        tree_weights, axis=-1, keepdims=True
    )
    cache_weights = (cache_weights / denominator).astype(jnp.bfloat16)
    tree_weights = (tree_weights / denominator).astype(jnp.bfloat16)
    result = jnp.einsum(
        "rhnc,rcd->rnhd", cache_weights, cache_values, preferred_element_type=jnp.float32
    )
    result = result + jnp.einsum(
        "rhnm,rmd->rnhd", tree_weights, tree_values, preferred_element_type=jnp.float32
    )
    return result.astype(jnp.bfloat16)


def refresh(logical_pages, length, leaf, reach, depth, new_keys, new_values):
    count = logical_pages.shape[0] * logical_pages.shape[2]
    logical = jnp.transpose(logical_pages, (1, 0, 2, 3)).reshape(2, count, HD)
    slot_ids = jnp.arange(count, dtype=jnp.int32)
    on_path = reach[leaf]
    selector = ((on_path[None, :] > 0.5) & (depth[None, :] == slot_ids[:, None] - length)).astype(
        jnp.float32
    )
    placed_keys = jnp.dot(selector, new_keys.astype(jnp.float32), precision=lax.Precision.HIGHEST)
    placed_values = jnp.dot(
        selector, new_values.astype(jnp.float32), precision=lax.Precision.HIGHEST
    )
    placed = jnp.stack([placed_keys, placed_values]).astype(jnp.bfloat16)
    written = jnp.sum(selector, axis=1) > 0.5
    logical = jnp.where(written[None, :, None], placed, logical)
    return jnp.transpose(
        logical.reshape(2, logical_pages.shape[0], logical_pages.shape[2], HD), (1, 0, 2, 3)
    )


def contract(source, piece):
    return jnp.dot(source, piece, preferred_element_type=jnp.float32)


def project_memory(rows, keyvalue_weight, position):
    projected = contract(rows, lax.all_gather(keyvalue_weight, "tok", axis=0, tiled=True))
    new_keys = rotate(projected[:, :HD], position).astype(jnp.bfloat16)
    new_values = projected[:, HD:].astype(jnp.bfloat16)
    return (new_keys, new_values)


def split_pages(page_blocks, count):
    cache_keys = page_blocks[:, :, 0].reshape(count, NPR * PAGE, HD)
    cache_values = page_blocks[:, :, 1].reshape(count, NPR * PAGE, HD)
    return (cache_keys, cache_values)


def reduce_heads(mixed, output_weight, safe_heads, head_mask, slots_per):
    head_count = lax.axis_size("head")
    tok_count = lax.axis_size("tok")
    narrow = output_weight.shape[1]
    blocks = lax.all_gather(output_weight, "head", axis=1, tiled=True)
    part_cols = blocks.shape[1]
    my_output_weight = (
        jnp.take(blocks.reshape(HQ, HD, part_cols), safe_heads, axis=0) * head_mask[:, None, None]
    )
    my_output_weight = my_output_weight.reshape(slots_per * HD, part_cols)
    partial_value = jnp.dot(
        mixed,
        lax.all_gather(my_output_weight, "tok", axis=1, tiled=True),
        preferred_element_type=jnp.float32,
    ).astype(jnp.bfloat16)
    row_count = partial_value.shape[0]
    partial_value = partial_value.reshape(row_count, tok_count, head_count, narrow)
    partial_value = jnp.transpose(partial_value, (0, 2, 1, 3)).reshape(
        row_count, tok_count * head_count * narrow
    )
    partial_value = lax.optimization_barrier(partial_value)
    summed = lax.psum_scatter(
        partial_value.astype(jnp.float32).astype(jnp.bfloat16),
        "head",
        scatter_dimension=1,
        tiled=True,
    )
    return summed


def shards(
    tokens,
    query_weight,
    keyvalue_weight,
    output_weight,
    cache,
    page_table,
    parents,
    cache_len,
    accepted_leaf,
):
    head_count = lax.axis_size("head")
    head_index = lax.axis_index("head")
    tok_index = lax.axis_index("tok")
    slots_per = -(-HQ // head_count)
    requests = parents.shape[0]
    owned = requests // head_count
    rows_owned = owned * DRAFT
    pages_dev = cache.shape[0]
    gathered = lax.all_gather(tokens, "head", axis=1, tiled=True)
    wide = gathered.astype(jnp.float32)
    mean_square = jnp.mean(wide * wide, axis=1, keepdims=True)
    normed = (wide * lax.rsqrt(mean_square + 1e-06)).astype(jnp.bfloat16)
    reach, depth = jax.vmap(ancestry)(parents)
    position = cache_len[:, None] + depth
    flat_pos = position.reshape(-1)
    head_ids = head_index + head_count * jnp.arange(slots_per, dtype=jnp.int32)
    usable = head_ids < HQ
    safe_heads = jnp.minimum(head_ids, HQ - 1)
    head_mask = usable.astype(jnp.bfloat16)
    part_rows = query_weight.shape[0]
    my_query_weight = (
        jnp.take(query_weight.reshape(part_rows, HQ, HD), safe_heads, axis=1)
        * head_mask[None, :, None]
    )
    my_query_weight = my_query_weight.reshape(part_rows, slots_per * HD)
    queries = contract(normed, lax.all_gather(my_query_weight, "tok", axis=0, tiled=True))
    queries = (rotate(queries.reshape(-1, slots_per, HD), flat_pos[:, None]) * HD ** (-0.5)).astype(
        jnp.bfloat16
    )
    own_start = head_index * rows_owned
    own_reach = lax.dynamic_slice_in_dim(reach, head_index * owned, owned, 0)
    own_depth = lax.dynamic_slice_in_dim(depth, head_index * owned, owned, 0)
    own_len = lax.dynamic_slice_in_dim(cache_len, head_index * owned, owned, 0)
    own_leaf = lax.dynamic_slice_in_dim(accepted_leaf, head_index * owned, owned, 0)
    device = tok_index * head_count + head_index
    own_table = (
        lax.dynamic_slice_in_dim(page_table, head_index * owned, owned, 0) - device * pages_dev
    )
    own_pages = jnp.take(cache, own_table.reshape(-1), axis=0).reshape(owned, NPR, 2, PAGE, HD)
    tree_keys, tree_values = project_memory(normed, keyvalue_weight, flat_pos)
    own_keys = lax.dynamic_slice_in_dim(tree_keys, own_start, rows_owned, 0)
    own_values = lax.dynamic_slice_in_dim(tree_values, own_start, rows_owned, 0)
    page_pool = lax.all_gather(cache, "head", axis=0, tiled=True)
    local_ids = page_table - tok_index * head_count * pages_dev
    page_blocks = jnp.take(page_pool, local_ids.reshape(-1), axis=0).reshape(
        requests, NPR, 2, PAGE, HD
    )
    cache_keys, cache_values = split_pages(page_blocks, requests)
    result = attend(
        queries.reshape(requests, DRAFT, slots_per, HD),
        cache_keys,
        cache_values,
        tree_keys.reshape(requests, DRAFT, HD),
        tree_values.reshape(requests, DRAFT, HD),
        cache_len,
        position,
        reach,
    )
    mixed = result.reshape(-1, slots_per * HD)
    attended = reduce_heads(mixed, output_weight, safe_heads, head_mask, slots_per)
    new_pages = jax.vmap(refresh)(
        own_pages,
        own_len,
        own_leaf,
        own_reach,
        own_depth,
        own_keys.reshape(owned, DRAFT, HD),
        own_values.reshape(owned, DRAFT, HD),
    )
    flat_ids = own_table.reshape(-1)
    matches = (flat_ids[:, None] == jnp.arange(pages_dev, dtype=jnp.int32)[None, :]).astype(
        jnp.int32
    )
    inverse = jnp.sum(matches * jnp.arange(pages_dev, dtype=jnp.int32)[:, None], axis=0)
    cache_out = jnp.take(new_pages.reshape(pages_dev, 2, PAGE, HD), inverse, axis=0)
    return (attended, cache_out)


def fused_kernel(
    tok_ref,
    qw_ref,
    kvw_ref,
    wo_ref,
    cache_ref,
    parents_ref,
    table_ref,
    len_ref,
    leaf_ref,
    out_ref,
    cache_out_ref,
    wbuf,
    obuf,
    xbuf,
    cbuf,
    kvbuf,
    qbuf,
    mixbuf,
    reach_buf,
    depth_buf,
    nbuf,
    accum,
    psend,
    pown,
    precv,
    fsend,
    final,
    y_send,
    y_recv,
    part_send,
    part_recv,
    final_send,
    final_recv,
    mix_send,
    mix_recv,
    load_sem,
    *piece_sems,
):
    tok_count = wbuf.shape[0]
    levels = tok_count // (XS * CORES)
    slots = qbuf.shape[0]
    rows = tok_ref.shape[0]
    narrow = wo_ref.shape[0]
    requests = parents_ref.shape[0]
    level = XS * CORES
    part_rows = wbuf.shape[1]
    qcols = slots * HD
    me = lax.axis_index("tok")
    y = lax.axis_index("head")
    other = 1 - y
    core = lax.rem(me, CORES)
    xpos = lax.rem(lax.div(me, CORES), XS)
    z = lax.div(me, CORES * XS)

    def tok_at(zz, xx, cc):
        return (zz * XS + xx) * CORES + cc

    up_dev = (jnp.minimum(me + XS * CORES, tok_count - 1), y)
    down_dev = (jnp.maximum(me - XS * CORES, 0), y)
    x_dev = (tok_at(z, 1 - xpos, core), y)
    core_dev = (tok_at(z, xpos, 1 - core), y)
    y_dev = (me, other)
    has_up = z < levels - 1
    has_down = z > 0

    def columns(slot, group):
        return pl.ds(pl.multiple_of((2 * slot + group) * HD, HD), HD)

    loads = [
        (
            qw_ref.at[:, columns(slot, y)],
            wbuf.at[me, :, slot * HD : (slot + 1) * HD],
        )
        for slot in range(slots)
    ]
    loads.append((kvw_ref.at[:, pl.ds(pl.multiple_of(y * HD, HD), HD)], wbuf.at[me, :, qcols:]))
    weight_loads = len(loads)
    loads += [
        (
            wo_ref.at[:, columns(slot, y)],
            obuf.at[y, me, :, slot * HD : (slot + 1) * HD],
        )
        for slot in range(slots)
    ]
    loads += [(tok_ref, xbuf.at[y]), (cache_ref, cbuf.at[y])]
    loads = [
        pltpu.make_async_copy(source, target, load_sem.at[index])
        for index, (source, target) in enumerate(loads)
    ]
    for load in loads:
        load.start()

    barrier = pltpu.get_barrier_semaphore()
    for device in (x_dev, core_dev, y_dev):
        pl.semaphore_signal(barrier, inc=1, device_id=device, device_id_type=MESH)

    @pl.when(has_up)
    def _():
        pl.semaphore_signal(barrier, inc=1, device_id=up_dev, device_id_type=MESH)

    @pl.when(has_down)
    def _():
        pl.semaphore_signal(barrier, inc=1, device_id=down_dev, device_id_type=MESH)

    pl.semaphore_wait(barrier, 3 + has_up.astype(jnp.int32) + has_down.astype(jnp.int32))

    def remote(source, target, send_sem, recv_sem, device):
        return pltpu.make_async_remote_copy(
            src_ref=source,
            dst_ref=target,
            send_sem=send_sem,
            recv_sem=recv_sem,
            device_id=device,
            device_id_type=MESH,
        )

    def each_level(distance, run):
        if distance == 0:
            run(z)
            return
        pl.when(z - distance >= 0)(lambda: run(z - distance))
        pl.when(z + distance < levels)(lambda: run(z + distance))

    class Piece:
        def __init__(self, view, sems, cross_x):
            self.view = view
            self.up, self.down, self.xs, self.cs, self.recv = sems
            self.cross_x = cross_x

        def copy(self, t, sems, device):
            ref = self.view(t)
            return remote(ref, ref, sems.at[lax.div(t, CORES)], self.recv.at[t], device)

        def along(self, t, act, up, down):
            if up:
                pl.when(has_up)(lambda: act(self.copy(t, self.up, up_dev)))
            if down:
                pl.when(has_down)(lambda: act(self.copy(t, self.down, down_dev)))

        def spread(self, t, own_x, act):
            if own_x and self.cross_x:
                act(self.copy(t, self.xs, x_dev))
            act(self.copy(t, self.cs, core_dev))

        def arrive(self, t):
            self.copy(t, self.cs, core_dev).wait_recv()

        def visit(self, distance, sending, act):
            def go(zz, up, down):
                t = tok_at(zz, xpos, core)
                if sending and distance:
                    self.arrive(t)
                self.along(t, act, up, down)
                self.spread(t, True, act)

            if distance == 0:
                go(z, True, True)
                return
            pl.when(z - distance >= 0)(lambda: go(z - distance, True, False))
            pl.when(z + distance < levels)(lambda: go(z + distance, False, True))

        def cross(self, distance, sending, act):
            if not self.cross_x:
                return

            def go(zz):
                t = tok_at(zz, 1 - xpos, core)
                if sending:
                    self.arrive(t)
                self.spread(t, False, act)

            each_level(distance, go)

        def step(self, distance):
            self.visit(distance, True, lambda copy: copy.start())

        def relay(self, distance):
            self.cross(distance, True, lambda copy: copy.start())

        def gathered(self, zz):
            self.arrive(tok_at(zz, xpos, 1 - core))
            if self.cross_x:
                self.arrive(tok_at(zz, 1 - xpos, 1 - core))

        def drain(self):
            for distance in range(levels):
                self.visit(distance, False, lambda copy: copy.wait_send())
                self.cross(distance, False, lambda copy: copy.wait_send())

    pieces = [piece_sems[5 * i : 5 * i + 5] for i in range(5)]
    cut = (slots + 1) // 3 * HD
    mid = (narrow // 2 + TILE - 1) // TILE * TILE
    weights = (
        Piece(lambda t: wbuf.at[t, :, :cut], pieces[0], True),
        Piece(lambda t: wbuf.at[t, :, cut : 2 * cut], pieces[1], True),
        Piece(lambda t: wbuf.at[t, :, 2 * cut :], pieces[4], True),
    )
    outputs = (
        Piece(lambda t: obuf.at[:, t, :mid], pieces[2], False),
        Piece(lambda t: obuf.at[:, t, mid:], pieces[3], False),
    )

    def step(group, distance):
        for piece in group:
            piece.step(distance)

    def relay(group, distance):
        for piece in group:
            piece.relay(distance)

    wosends = [
        remote(
            wo_ref.at[:, columns(slot, other)],
            obuf.at[y, me, :, slot * HD : (slot + 1) * HD],
            y_send.at[3 + slot],
            y_recv.at[3 + slot],
            y_dev,
        )
        for slot in range(slots)
    ]
    xsend = remote(tok_ref, xbuf.at[y], y_send.at[0], y_recv.at[0], y_dev)
    csend = remote(cache_ref, cbuf.at[y], y_send.at[1], y_recv.at[1], y_dev)
    for copy in wosends + [xsend]:
        copy.start()
    for load in loads[:weight_loads]:
        load.wait()
    step(weights, 0)
    csend.start()
    for load in loads[weight_loads:]:
        load.wait()

    row_ids = lax.broadcasted_iota(jnp.int32, (DRAFT, DRAFT), 0)
    col_ids = lax.broadcasted_iota(jnp.int32, (DRAFT, DRAFT), 1)
    eye = (row_ids == col_ids).astype(jnp.float32)
    lane = lax.broadcasted_iota(jnp.int32, (1, HD // 2), 1)
    quarter = HD // 4
    pair = jnp.where(lane < quarter, lane, lane - quarter).astype(jnp.float32)
    freq = jnp.exp(pair * (-2.0 * math.log(10000.0) / (HD // 2)))
    sign = jnp.where(lane < quarter, -1.0, 1.0)
    reaches = []
    positions = []
    for r in range(requests):
        back = (row_ids == parents_ref[r : r + 1, :]).astype(jnp.float32)
        back = jnp.minimum(back + eye, 1.0)
        for sweep in range((DRAFT - 1).bit_length()):
            low = back.astype(jnp.bfloat16)
            back = jnp.minimum(jnp.dot(low, low, preferred_element_type=jnp.float32), 1.0)
        reach = lax.dot_general(
            eye.astype(jnp.bfloat16),
            back.astype(jnp.bfloat16),
            NT,
            preferred_element_type=jnp.float32,
        )
        reach_buf[r] = reach
        depth_buf[r] = jnp.sum(back, axis=0, keepdims=True) - 1.0
        reaches.append(reach)
        depth = jnp.sum(reach, axis=1, keepdims=True) - 1.0
        positions.append(depth + len_ref[r].astype(jnp.float32))
    angle = jnp.concatenate(positions, axis=0) * freq
    cosine = jnp.cos(angle)
    sine = jnp.sin(angle) * sign

    def rotated(value):
        turn = value[:, : HD // 2]
        swapped = jnp.concatenate([turn[:, quarter:], turn[:, :quarter]], axis=1)
        return jnp.concatenate([turn * cosine + swapped * sine, value[:, HD // 2 :]], axis=1)

    xsend.wait_recv()
    wide = jnp.concatenate([xbuf[0], xbuf[1]], axis=1).astype(jnp.float32)
    mean_square = jnp.mean(wide * wide, axis=1, keepdims=True)
    nbuf[...] = (wide * lax.rsqrt(mean_square + 1e-06)).astype(jnp.bfloat16)
    span_rows = level * part_rows

    def project(distance):
        def run(zz):
            for piece in weights:
                piece.gathered(zz)
            source = nbuf[:, pl.ds(pl.multiple_of(zz * span_rows, 128), span_rows)]
            for slot in range(slots + 1):
                at = slice(slot * HD, (slot + 1) * HD)
                block = wbuf[pl.ds(zz * level, level), :, at].reshape(span_rows, HD)
                part = jnp.dot(source, block, preferred_element_type=jnp.float32)
                if distance == 0:
                    accum[:, at] = part
                else:
                    accum[:, at] += part

        each_level(distance, run)

    step(weights, 1)
    relay(weights, 0)
    project(0)
    step(weights, 2)
    relay(weights, 1)
    for copy in wosends:
        copy.wait_recv()
    step(outputs, 0)
    project(1)
    for distance in range(3, levels):
        step(weights, distance)
        relay(weights, distance - 1)
        if distance == 3:
            step(outputs, 1)
        project(distance - 1)
    relay(weights, levels - 1)
    project(levels - 1)

    projected = accum[:, qcols:]

    @pl.when(y == 0)
    def _():
        kvbuf[0] = rotated(projected).astype(jnp.bfloat16)

    @pl.when(y == 1)
    def _():
        kvbuf[1] = projected.astype(jnp.bfloat16)

    kvsend = remote(kvbuf.at[y], kvbuf.at[y], y_send.at[2], y_recv.at[2], y_dev)
    kvsend.start()
    step(outputs, 2)
    for slot in range(slots):
        value = rotated(accum[:, slot * HD : (slot + 1) * HD])
        qbuf[slot] = (value * HD ** (-0.5)).astype(jnp.bfloat16)
    kvsend.wait_recv()
    csend.wait_recv()

    def attend_one(r):
        span = slice(r * DRAFT, (r + 1) * DRAFT)
        queries = qbuf[:, span, :].reshape(slots * DRAFT, HD)
        ids = [lax.rem(table_ref[r, j], NPR) for j in range(NPR)]
        keys = jnp.concatenate([cbuf[r, i, 0] for i in ids], axis=0)
        values = jnp.concatenate([cbuf[r, i, 1] for i in ids], axis=0)
        span_len = NPR * PAGE
        slot_ids = lax.broadcasted_iota(jnp.int32, (DRAFT, span_len), 1)
        first = positions[r].astype(jnp.int32) - WINDOW
        visible = (slot_ids < len_ref[r]) & (slot_ids > first)
        cache_bias = jnp.where(visible, 0.0, -1e30)
        tree_bias = jnp.where(reaches[r] > 0.5, 0.0, -1e30)
        scores = lax.dot_general(queries, keys, NT, preferred_element_type=jnp.float32)
        tree = lax.dot_general(queries, kvbuf[0, span, :], NT, preferred_element_type=jnp.float32)
        scores = jnp.where(cache_bias[None] < 0.0, -1e30, scores.reshape(slots, DRAFT, span_len))
        tree = jnp.where(tree_bias[None] < 0.0, -1e30, tree.reshape(slots, DRAFT, DRAFT))
        peak = jnp.maximum(
            jnp.max(scores, axis=-1, keepdims=True), jnp.max(tree, axis=-1, keepdims=True)
        )
        scores = jnp.exp(scores - peak)
        tree = jnp.exp(tree - peak)
        total = jnp.sum(scores, axis=-1, keepdims=True) + jnp.sum(tree, axis=-1, keepdims=True)
        scores = (scores / total).astype(jnp.bfloat16).reshape(slots * DRAFT, span_len)
        tree = (tree / total).astype(jnp.bfloat16).reshape(slots * DRAFT, DRAFT)
        result = jnp.dot(scores, values, preferred_element_type=jnp.float32)
        result = result + jnp.dot(tree, kvbuf[1, span, :], preferred_element_type=jnp.float32)
        result = result.astype(jnp.bfloat16)
        for slot in range(slots):
            mixbuf[xpos, span, slot * HD : (slot + 1) * HD] = result[slot * DRAFT : (slot + 1) * DRAFT]

    def refresh_one():
        length = len_ref[y]
        own_reach = reach_buf[y]
        on_path = jnp.sum(jnp.where(row_ids == leaf_ref[y], own_reach, 0.0), axis=0, keepdims=True)
        depth_row = depth_buf[y].astype(jnp.int32)
        keep = pl.ds(pl.multiple_of(y * DRAFT, DRAFT), DRAFT)
        new_keys = kvbuf[0, keep, :]
        new_values = kvbuf[1, keep, :]
        slot_ids = lax.broadcasted_iota(jnp.int32, (PAGE, DRAFT), 0)
        for page in range(NPR):
            logical = jnp.int32(0)
            for j in range(1, NPR):
                logical = logical + jnp.where(lax.rem(table_ref[y, j], NPR) == page, j, 0)
            chosen = (on_path > 0.5) & (depth_row == slot_ids + (logical * PAGE - length))
            selector = chosen.astype(jnp.float32)
            written = jnp.sum(selector, axis=1, keepdims=True) > 0.5
            selector = selector.astype(jnp.bfloat16)
            for entry, new in ((0, new_keys), (1, new_values)):
                placed = jnp.dot(selector, new, preferred_element_type=jnp.float32)
                old = cbuf[y, page, entry].astype(jnp.float32)
                cache_out_ref[page, entry] = jnp.where(written, placed, old).astype(jnp.bfloat16)

    width = CORES * narrow

    def part_copy(zz):
        return remote(psend.at[zz], precv.at[zz], part_send.at[zz], part_recv.at[zz], y_dev)

    def final_copy(zz):
        ref = final.at[xpos, zz]
        return remote(fsend.at[zz], ref, final_send.at[zz], final_recv.at[zz], x_dev)

    def mix_copy(r):
        ref = mixbuf.at[xpos, r * DRAFT : (r + 1) * DRAFT]
        return remote(ref, ref, mix_send.at[r], mix_recv.at[r], x_dev)

    def output_level(zz):
        for piece in outputs:
            piece.gathered(zz)
        mixed = mixbuf[...].reshape(XS * rows, qcols)
        own = pl.ds(zz * level + xpos * CORES, CORES)
        block = obuf[other, own].reshape(width, qcols)
        value = lax.dot_general(mixed, block, NT, preferred_element_type=jnp.float32)
        psend[zz] = value.astype(jnp.bfloat16).reshape(XS, rows, width)
        part_copy(zz).start()
        block = obuf[y, own].reshape(width, qcols)
        value = lax.dot_general(mixed, block, NT, preferred_element_type=jnp.float32)
        pown[zz] = value.astype(jnp.bfloat16).reshape(XS, rows, width)

    def sum_level(zz):
        part_copy(zz).wait_recv()

        def summed(xx):
            total = pown[zz, xx].astype(jnp.float32) + precv[zz, xx].astype(jnp.float32)
            return total.astype(jnp.bfloat16)

        fsend[zz] = summed(1 - xpos)
        final_copy(zz).start()
        final[xpos, zz] = summed(xpos)

    attend_one(0)
    mix_copy(0).start()
    for distance in range(3, levels):
        step(outputs, distance)
    for r in range(1, requests):
        attend_one(r)
        mix_copy(r).start()
    for r in range(requests):
        mix_copy(r).wait_recv()
    for distance in range(levels):
        each_level(distance, output_level)
        if distance > 0:
            each_level(distance - 1, sum_level)
    refresh_one()
    each_level(levels - 1, sum_level)
    for zz in range(levels):
        final_copy(zz).wait_recv()
    done = [final[xx, zz] for zz in range(levels) for xx in range(XS)]
    out_ref[...] = jnp.concatenate(done, axis=1)
    for piece in weights + outputs:
        piece.drain()
    for copy in [xsend, csend, kvsend] + wosends + [mix_copy(r) for r in range(requests)]:
        copy.wait_send()
    for zz in range(levels):
        part_copy(zz).wait_send()
        final_copy(zz).wait_send()


def fused(tokens, query_weight, keyvalue_weight, output_weight, cache, page_table, parents, cache_len, accepted_leaf):
    tok_count = lax.axis_size("tok")
    heads = lax.axis_size("head")
    slots = HQ // heads
    rows, half = tokens.shape
    part_rows = query_weight.shape[0]
    narrow = output_weight.shape[1]
    requests = parents.shape[0]
    pages = cache.shape[0]
    qcols = slots * HD
    positions = tok_count // CORES
    levels = positions // XS
    hbm = pl.BlockSpec(memory_space=pltpu.HBM)
    vmem = pl.BlockSpec(memory_space=pltpu.VMEM)
    smem = pl.BlockSpec(memory_space=pltpu.SMEM)
    bf16 = jnp.bfloat16
    scratch = [
        pltpu.VMEM((tok_count, part_rows, qcols + HD), bf16),
        pltpu.VMEM((heads, tok_count, narrow, qcols), bf16),
        pltpu.VMEM((heads, rows, half), bf16),
        pltpu.VMEM((heads,) + cache.shape, bf16),
        pltpu.VMEM((2, rows, HD), bf16),
        pltpu.VMEM((slots, rows, HD), bf16),
        pltpu.VMEM((XS, rows, qcols), bf16),
        pltpu.VMEM((requests, DRAFT, DRAFT), jnp.float32),
        pltpu.VMEM((requests, 1, DRAFT), jnp.float32),
        pltpu.VMEM((rows, half * heads), bf16),
        pltpu.VMEM((rows, qcols + HD), jnp.float32),
        pltpu.VMEM((levels, XS, rows, CORES * narrow), bf16),
        pltpu.VMEM((levels, XS, rows, CORES * narrow), bf16),
        pltpu.VMEM((levels, XS, rows, CORES * narrow), bf16),
        pltpu.VMEM((levels, rows, CORES * narrow), bf16),
        pltpu.VMEM((XS, levels, rows, CORES * narrow), bf16),
        pltpu.SemaphoreType.DMA((3 + slots,)),
        pltpu.SemaphoreType.DMA((3 + slots,)),
        pltpu.SemaphoreType.DMA((levels,)),
        pltpu.SemaphoreType.DMA((levels,)),
        pltpu.SemaphoreType.DMA((levels,)),
        pltpu.SemaphoreType.DMA((levels,)),
        pltpu.SemaphoreType.DMA((requests,)),
        pltpu.SemaphoreType.DMA((requests,)),
        pltpu.SemaphoreType.DMA((2 * slots + 3,)),
    ]
    for piece in range(5):
        scratch += [pltpu.SemaphoreType.DMA((positions,))] * 4
        scratch += [pltpu.SemaphoreType.DMA((tok_count,))]
    return pl.pallas_call(
        fused_kernel,
        out_shape=(
            jax.ShapeDtypeStruct(tokens.shape, bf16),
            jax.ShapeDtypeStruct(cache.shape, bf16),
        ),
        in_specs=[hbm] * 5 + [vmem] + [smem] * 3,
        out_specs=(vmem, vmem),
        scratch_shapes=scratch,
        compiler_params=pltpu.CompilerParams(
            collective_id=0, has_side_effects=True, vmem_limit_bytes=64 * 1024 * 1024
        ),
        cost_estimate=pl.CostEstimate(
            flops=4 * rows * HD * HQ * HD * 5, bytes_accessed=1 << 22, transcendentals=1 << 19
        ),
    )(
        tokens,
        query_weight,
        keyvalue_weight,
        jnp.transpose(output_weight),
        cache,
        parents,
        page_table,
        cache_len,
        accepted_leaf,
    )


def fits(tok_count, head_count, args):
    tokens, query_weight, _, output_weight, cache, _, parents, _, _ = args
    return (
        head_count == 2
        and tok_count % (2 * XS * CORES) == 0
        and tok_count >= 3 * XS * CORES
        and query_weight.shape[0] % TILE == 0
        and output_weight.shape[1] % TILE == 0
        and output_weight.shape[1] >= 3 * TILE
        and XS * CORES * query_weight.shape[0] % 128 == 0
        and cache.shape[0] == NPR
        and parents.shape[0] == head_count
    )


def dispatch(*args):
    if fits(lax.axis_size("tok"), lax.axis_size("head"), args):
        return fused(*args)
    return shards(*args)


def solution(mesh):
    in_specs = (
        P("tok", "head"),
        P("tok", None),
        P("tok", None),
        P(None, ("head", "tok")),
        P(("tok", "head"), None, None, None),
        P("tok", None),
        P("tok", None),
        P("tok"),
        P("tok"),
    )
    out_specs = (P("tok", "head"), P(("tok", "head"), None, None, None))
    return jax.shard_map(
        dispatch, mesh=mesh, in_specs=in_specs, out_specs=out_specs, check_vma=False
    )
```
